128 devices in a mesh: student: 16 (over x, z_hi, core), pool: 8 (over z_lo, y).
Axes of the slice: x: 4, y: 4, z: 4 (z_hi: 2, z_lo: 2; z = z_hi * 2 + z_lo), core: 2. Of those that a mesh axis runs over, the one named last changes fastest.
Arguments:
- pixels: bfloat16 [512, 128, 588], P(('student', 'pool')), may hold values from -6 to 6
- keyframes: int32 [128, 2], P(('student', 'pool')), may hold values from 0 to 3, as said below
- destination: int32 [128, 2], P(('student', 'pool')), may hold values from 0 to 7, as said below
- student_embed: float32 [588, 384], replicated, may hold values from -0.25 to 0.25
- student_gain: float32 [384], replicated, may hold values from 0.1 to 1.9
- student_up: float32 [384, 1536], replicated, may hold values from -0.3125 to 0.3125
- student_down: float32 [1536, 384], replicated, may hold values from -0.15625 to 0.15625
- student_head: float32 [384, 1536], replicated, may hold values from -0.3125 to 0.3125
- teacher_embed: bfloat16 [8, 588, 1536], P('pool', None, 'student'), may hold values from -0.25 to 0.25
- teacher_gain: float32 [8, 1536], P('pool'), may hold values from 0.1 to 1.9
- teacher_project: bfloat16 [8, 1536, 4608], P('pool', None, 'student'), may hold values from -1.8371173 to 1.8371173
- teacher_output: bfloat16 [8, 1536, 1536], P('pool', None, 'student'), may hold values from -0.15625 to 0.15625
Outputs:
- mean_distance: float32 [], replicated
- grad_embed: float32 [588, 384], replicated
- grad_gain: float32 [384], replicated
- grad_up: float32 [384, 1536], replicated
- grad_down: float32 [1536, 384], replicated
- grad_head: float32 [384, 1536], replicated
The draws below stay inside these ranges and needn't reach their ends.
Inputs may be any that keep to these rules, and one draw needn't show every extreme that they name: `keyframes`: the 2 indices of one device are distinct. `destination`: the 2 teachers of one device are distinct. Among the 8 devices with one student index, some teacher is assigned a block by every one of them.
All inputs are finite; a program needn't handle non-finite values.
Results may differ from the reference program's by a relative error of at most 0.008.
Values may be sent and summed in bfloat16 or wider, within the bound.
No kernel may reach another device: no remote copies, remote signals or barrier semaphores. Data moves between devices by JAX's collectives and lax.ppermute only.
A program may use at most 192 MiB of HBM per device.

```python
import jax
import jax.numpy as jnp
from jax import lax

HEADS = 24
HDIM = 64
D_T = 1536
D_S = 384
S_HID = 1536
PIX = 588
BLK = 128
NBLK = 4
KEY = 2
BLOCKS = 512
N_POOL = 8
DEVICES = 128


def draw_keyframes(key, part):
    key = jax.random.fold_in(key, 3)
    scores = jax.random.randint(key, (DEVICES, NBLK), 0, 1 << 20) * NBLK + jnp.arange(NBLK, dtype=jnp.int32)[None, :]
    order = jnp.argsort(scores, axis=1, stable=True)
    return order[:, :KEY].astype(jnp.int32)


def draw_destination(key, part):
    key = jax.random.fold_in(key, 5)
    groups = DEVICES // N_POOL
    favoured = jax.random.randint(jax.random.fold_in(key, 1), (groups, 1), 0, N_POOL)
    favoured = jnp.repeat(favoured, N_POOL, axis=0)
    columns = jnp.arange(N_POOL, dtype=jnp.int32)[None, :]
    scores = jax.random.randint(jax.random.fold_in(key, 2), (DEVICES, N_POOL), 0, 1 << 20) * N_POOL + columns
    scores = jnp.where(columns == favoured, -1, scores)
    order = jnp.argsort(scores, axis=1, stable=True)[:, :KEY]
    turned = jax.random.randint(jax.random.fold_in(key, 3), (DEVICES, 1), 0, KEY)
    places = (jnp.arange(KEY, dtype=jnp.int32)[None, :] + turned) % KEY
    return jnp.take_along_axis(order, places, axis=1).astype(jnp.int32)


def draw_teacher_project(key, part):
    key = jax.random.fold_in(key, 7)
    width = HEADS * HDIM
    base = jnp.clip(jax.random.normal(key, (N_POOL, width, 3 * width), jnp.float32), -6.0, 6.0) * width ** (-0.5)
    return base.astype(jnp.bfloat16)


def level_of(rng, extent, shards, low, largest):
    level = 1.0
    for axis_at, blocks in shards:
        steps = jax.random.uniform(jax.random.fold_in(jax.random.fold_in(rng, 6), axis_at), (blocks,), jnp.float32, low / len(shards), largest / len(shards))
        level = level * jnp.repeat(jnp.exp(steps), extent[axis_at] // blocks).reshape((-1,) + (1,) * (len(extent) - 1 - axis_at))
    return level


def scatter_about(stream_key, dims, deviation, bound, pieces=(), kind=jnp.bfloat16):
    array = deviation * jax.random.normal(stream_key, dims, jnp.float32)
    if pieces:
        array = array * level_of(stream_key, dims, pieces, -0.22, 0.18)
    return jnp.clip(array, -bound, bound).astype(kind)


def setup_inputs(seed: int = 0) -> dict:
    arg_keys = jax.random.split(jax.random.key(seed), 13)
    return {
        "pixels": scatter_about(arg_keys[0], (BLOCKS, BLK, PIX), 1.0, 6.0, ((0, 128),)),
        "keyframes": draw_keyframes(jax.random.fold_in(arg_keys[12], 71), 0),
        "destination": draw_destination(jax.random.fold_in(arg_keys[12], 71), 0),
        "student_embed": scatter_about(arg_keys[3], (PIX, D_S), PIX ** -0.5, 0.25, (), jnp.float32),
        "student_gain": jnp.clip(1.0 + 0.18 * jax.random.normal(arg_keys[4], (D_S,), jnp.float32), 0.1, 1.9),
        "student_up": scatter_about(arg_keys[5], (D_S, S_HID), D_S ** -0.5, 0.3125, (), jnp.float32),
        "student_down": scatter_about(arg_keys[6], (S_HID, D_S), S_HID ** -0.5, 0.15625, (), jnp.float32),
        "student_head": scatter_about(arg_keys[7], (D_S, D_T), D_S ** -0.5, 0.3125, (), jnp.float32),
        "teacher_embed": scatter_about(arg_keys[8], (N_POOL, PIX, D_T), PIX ** -0.5, 0.25, ((0, 8), (2, 16))),
        "teacher_gain": jnp.clip(1.0 + 0.18 * jax.random.normal(arg_keys[9], (N_POOL, D_T), jnp.float32), 0.1, 1.9),
        "teacher_project": draw_teacher_project(jax.random.fold_in(arg_keys[12], 71), 0),
        "teacher_output": scatter_about(arg_keys[11], (N_POOL, D_T, D_T), D_T ** -0.5, 0.15625, ((0, 8), (2, 16))),
    }


EPSILON = 1e-06

def product(left, right):
    return jnp.dot(left, right, precision=lax.Precision.HIGHEST)

def rms_scale(values):
    return lax.rsqrt(lax.optimization_barrier(jnp.mean(values * values, axis=-1, keepdims=True)) + EPSILON)

def student_trunk(embed, gain, upward, downward, rows):
    lifted = product(rows, embed)
    normed = lifted * rms_scale(lifted) * gain
    return lifted + product(jax.nn.gelu(product(normed, upward), approximate=False), downward)

def distance_total(head, hidden, target):
    student_out = product(hidden, head)
    cosine = lax.optimization_barrier(jnp.mean(student_out * target, axis=-1)) * rms_scale(student_out)[..., 0] * rms_scale(target)[..., 0]
    return jnp.sum(1.0 - cosine)

def teacher_block(block, embed, gain, project, output):
    high = lax.Precision.HIGHEST
    embedded = jnp.einsum('sbp,pd->sbd', block.astype(jnp.float32), embed.astype(jnp.float32), precision=high)
    normed = (embedded * rms_scale(embedded) * gain).astype(jnp.bfloat16)
    mixed = jnp.einsum('sbd,de->sbe', normed.astype(jnp.float32), project.astype(jnp.float32), precision=high).astype(jnp.bfloat16)
    slots, width, total = mixed.shape
    parts = mixed.reshape(slots, width, 3, HEADS, HDIM).astype(jnp.float32)
    scores = jnp.einsum('sqhd,skhd->shqk', parts[:, :, 0], parts[:, :, 1], precision=high) * HDIM ** (-0.5)
    weights = jax.nn.softmax(scores, axis=-1).astype(jnp.bfloat16).astype(jnp.float32)
    context = jnp.einsum('shqk,skhd->sqhd', weights, parts[:, :, 2], precision=high)
    context = context.astype(jnp.bfloat16).reshape(slots, width, HEADS * HDIM).astype(jnp.float32)
    finished = embedded + jnp.einsum('sbd,de->sbe', context, output.astype(jnp.float32), precision=high)
    return (finished * rms_scale(finished)).astype(jnp.bfloat16)

def reference(pixels, keyframes, destination, student_embed, student_gain, student_up, student_down, student_head, teacher_embed, teacher_gain, teacher_project, teacher_output):
    device_ids = jnp.arange(DEVICES, dtype=jnp.int32)[:, None]
    block_ids = (device_ids * NBLK + keyframes.astype(jnp.int32)).reshape(-1).astype(jnp.int32)
    owners = destination.reshape(-1).astype(jnp.int32)

    def one_block(item):
        block_id, owner = item
        block = lax.dynamic_index_in_dim(pixels, block_id, 0, keepdims=True)
        return teacher_block(block, teacher_embed[owner], teacher_gain[owner], teacher_project[owner], teacher_output[owner])[0]
    features = lax.map(one_block, (block_ids, owners))
    target = features.astype(jnp.float32).reshape(-1, HEADS * HDIM)
    rows = pixels[block_ids].astype(jnp.float32).reshape(-1, PIX)

    def total_of(embed, gain, upward, downward, head):
        hidden = student_trunk(embed, gain, upward, downward, rows)
        return distance_total(head, hidden, target)
    total, grads = jax.value_and_grad(total_of, argnums=(0, 1, 2, 3, 4))(student_embed, student_gain, student_up, student_down, student_head)
    mean_distance = total / (DEVICES * KEY * BLK)
    return (mean_distance, grads[0], grads[1], grads[2], grads[3], grads[4])
```

```python
import jax
import jax.numpy as jnp
from jax import lax
from jax.experimental import pallas as pl
from jax.experimental.pallas import tpu as pltpu
from jax.sharding import PartitionSpec as P

HEADS = 24
HDIM = 64
EPSILON = 1e-06
BOTH = ("student", "pool")
DEVICES = 128
PAIR = 2 * HDIM
LANES = 128
PIX = 588
PIX_PAD = 640
D_S = 384
D_T = 1536
S_HID = 1536
BLK = 128
HALF_ROWS = 8192
CHUNK = 128
NT = (((1,), (1,)), ((), ()))
TN = (((0,), (0,)), ((), ()))
NN = (((1,), (0,)), ((), ()))


def f32_dot(left, right, dims):
    return lax.dot_general(
        left, right, dims, precision=lax.Precision.HIGH, preferred_element_type=jnp.float32
    )


def bf16_dot(left, right, dims):
    return lax.dot_general(left, right, dims, preferred_element_type=jnp.float32)


def rms_scale(values):
    return lax.rsqrt(jnp.mean(values * values, axis=-1, keepdims=True) + EPSILON)


def attention_kernel(mixed_ref, out_ref):
    lane = lax.broadcasted_iota(jnp.int32, (BLK, PAIR), 1)
    first = lane < HDIM
    zero = jnp.zeros((BLK, PAIR), jnp.bfloat16)
    ones = jnp.concatenate(
        [jnp.where(first, 1.0, 0.0), jnp.where(first, 0.0, 1.0)], axis=0
    ).astype(jnp.bfloat16)
    for pair in range(HEADS // 2):
        at = pair * PAIR
        queries = mixed_ref[:, at : at + PAIR]
        keys = mixed_ref[:, D_T + at : D_T + at + PAIR]
        values = mixed_ref[:, 2 * D_T + at : 2 * D_T + at + PAIR]
        keys_two = jnp.concatenate(
            [jnp.where(first, keys, zero), jnp.where(first, zero, keys)], axis=0
        )
        values_two = jnp.concatenate(
            [jnp.where(first, values, zero), jnp.where(first, zero, values)], axis=0
        )
        scores = bf16_dot(queries, keys_two, NT)
        left, right = scores[:, :BLK], scores[:, BLK:]
        scale = HDIM ** (-0.5)
        left = jnp.exp((left - jnp.max(left, axis=1, keepdims=True)) * scale)
        right = jnp.exp((right - jnp.max(right, axis=1, keepdims=True)) * scale)
        weights = jnp.concatenate([left, right], axis=1).astype(jnp.bfloat16)
        summed = bf16_dot(weights, jnp.concatenate([values_two, ones], axis=1), NN)
        out_ref[:, at : at + PAIR] = (summed[:, :PAIR] / summed[:, PAIR:]).astype(jnp.bfloat16)


def attend(mixed):
    rows, total = mixed.shape
    return pl.pallas_call(
        attention_kernel,
        grid=(rows // BLK,),
        in_specs=[pl.BlockSpec((BLK, total), lambda b: (b, 0))],
        out_specs=pl.BlockSpec((BLK, D_T), lambda b: (b, 0)),
        out_shape=jax.ShapeDtypeStruct((rows, D_T), jnp.bfloat16),
        compiler_params=pltpu.CompilerParams(vmem_limit_bytes=32 * 1024 * 1024),
        cost_estimate=pl.CostEstimate(
            flops=rows * BLK * D_T * 8, bytes_accessed=rows * D_T * 8, transcendentals=rows * BLK * HEADS
        ),
        name="attention",
    )(mixed)


def core_groups():
    groups = [[], []]
    for device in range(DEVICES):
        groups[(device // 8) % 2].append(device)
    return groups


def core_swap(values):
    pairs = [(d, d ^ 8) for d in range(DEVICES)]
    return lax.ppermute(values, BOTH, pairs)


def to_lanes(grad):
    rows, columns = grad.shape
    return grad.reshape(rows, columns // LANES, LANES).transpose(1, 0, 2).reshape(-1, LANES)


def from_lanes(lanes, rows, columns):
    return lanes.reshape(columns // LANES, rows, LANES).transpose(1, 0, 2).reshape(rows, columns)


def split_three(value):
    first = lax.reduce_precision(value, 8, 7)
    second = lax.reduce_precision(value - first, 8, 7)
    return first, second, value - first - second


def sum_everywhere(grads, gain, total):
    parts = split_three(total)
    lane = lax.broadcasted_iota(jnp.int32, (1, LANES), 1)
    total_row = sum(jnp.where(lane == i, part, 0.0) for i, part in enumerate(parts))
    pieces = [to_lanes(grad) for grad in grads] + [gain.reshape(-1, LANES)]
    used = sum(piece.shape[0] for piece in pieces)
    flat = jnp.concatenate(
        pieces + [jnp.zeros((2 * HALF_ROWS - used - 1, LANES), jnp.float32), total_row], axis=0
    )
    core = lax.rem(lax.axis_index("student"), 2)
    halves = flat.reshape(2, HALF_ROWS, LANES)
    mine = lax.dynamic_index_in_dim(halves, core, 0, keepdims=False)
    other = lax.dynamic_index_in_dim(halves, 1 - core, 0, keepdims=False)
    mine = mine + core_swap(other)
    groups = core_groups()
    ranks = DEVICES // 2
    sent = mine.astype(jnp.bfloat16).reshape(ranks, CHUNK, LANES)
    got = lax.all_to_all(sent, BOTH, 0, 0, axis_index_groups=groups, tiled=True)
    chunk = jnp.sum(got.astype(jnp.float32), axis=0)
    rank = (lax.axis_index("student") // 2) * 8 + lax.axis_index("pool")
    last = jnp.logical_and(core == 1, rank == ranks - 1)
    again = split_three(jnp.sum(chunk[CHUNK - 1, :3]))
    again_row = sum(jnp.where(lane == i, part, 0.0) for i, part in enumerate(again))
    at_last = lax.broadcasted_iota(jnp.int32, (CHUNK, LANES), 0) == CHUNK - 1
    chunk = jnp.where(jnp.logical_and(last, at_last), again_row, chunk).astype(jnp.bfloat16)
    spread = jnp.broadcast_to(chunk[None], (ranks, CHUNK, LANES))
    half = lax.all_to_all(spread, BOTH, 0, 0, axis_index_groups=groups, tiled=True)
    half = half.reshape(HALF_ROWS, LANES)
    theirs = core_swap(half)
    low = jnp.where(core == 0, half, theirs)
    high = jnp.where(core == 0, theirs, half)
    flat = jnp.concatenate([low, high], axis=0).astype(jnp.float32)
    out, at = [], 0
    for grad in grads:
        rows, columns = grad.shape
        count = rows * columns // LANES
        out.append(from_lanes(flat[at : at + count], rows, columns))
        at += count
    gain_sum = flat[at : at + D_S // LANES].reshape(D_S)
    return out, gain_sum, jnp.sum(flat[-1, :3])


def on_device(
    pixels,
    keyframes,
    destination,
    student_embed,
    student_gain,
    student_up,
    student_down,
    student_head,
    teacher_embed,
    teacher_gain,
    teacher_project,
    teacher_output,
):
    pool_size = lax.axis_size("pool")

    def gathered(shard):
        return lax.all_gather(shard, "student", axis=0, tiled=True)

    embed_full = gathered(jnp.pad(teacher_embed[0].T, ((0, 0), (0, PIX_PAD - PIX))))
    project_full = gathered(teacher_project[0].T)
    output_full = gathered(teacher_output[0].T)

    teachers = jnp.arange(pool_size, dtype=jnp.int32)[:, None, None]
    chosen = [
        lax.dynamic_index_in_dim(pixels, keyframes[0, k], 0, keepdims=True) for k in range(2)
    ]
    outgoing = jnp.where(
        destination[0, 0] == teachers,
        chosen[0],
        jnp.where(destination[0, 1] == teachers, chosen[1], jnp.zeros((), jnp.bfloat16)),
    )
    outgoing = jnp.pad(outgoing, ((0, 0), (0, 0), (0, PIX_PAD - PIX)))
    arrived = lax.all_to_all(outgoing, "pool", split_axis=0, concat_axis=0, tiled=True)
    rows = arrived.reshape(pool_size * BLK, PIX_PAD)

    rows_f32 = rows.astype(jnp.float32)
    embed = jnp.pad(student_embed, ((0, PIX_PAD - PIX), (0, 0)))
    lifted = f32_dot(rows_f32, embed, NN)
    scale = rms_scale(lifted)
    unit = lifted * scale
    normed_s = unit * student_gain
    pre = f32_dot(normed_s, student_up, NN)
    cdf = 0.5 * (1.0 + lax.erf(pre * (2.0**-0.5)))
    act = pre * cdf
    slope = cdf + pre * jnp.exp(-0.5 * pre * pre) * ((2.0 * jnp.pi) ** -0.5)
    hidden = lifted + f32_dot(act, student_down, NN)
    student_out = f32_dot(hidden, student_head, NN)
    out_scale = rms_scale(student_out)

    embedded = bf16_dot(rows, embed_full, NT)
    normed = (embedded * rms_scale(embedded) * teacher_gain[0]).astype(jnp.bfloat16)
    mixed = bf16_dot(normed, project_full, NT).astype(jnp.bfloat16)
    context = attend(mixed)
    finished = embedded + bf16_dot(context, output_full, NT)
    features = (finished * rms_scale(finished)).astype(jnp.bfloat16).astype(jnp.float32)

    dot_mean = jnp.mean(student_out * features, axis=-1, keepdims=True)
    feature_scale = rms_scale(features)
    cosine = dot_mean * out_scale * feature_scale
    total = jnp.sum(cosine)
    along = -(feature_scale * out_scale) * (1.0 / D_T)
    back = (feature_scale * dot_mean * out_scale * out_scale * out_scale) * (1.0 / D_T)
    d_out = along * features + back * student_out
    grad_head = f32_dot(hidden, d_out, TN)
    d_hidden = f32_dot(d_out, student_head, NT)
    grad_down = f32_dot(act, d_hidden, TN)
    d_pre = f32_dot(d_hidden, student_down, NT) * slope
    grad_up = f32_dot(normed_s, d_pre, TN)
    d_normed = f32_dot(d_pre, student_up, NT)
    grad_gain = jnp.sum(d_normed * unit, axis=0)
    d_unit = d_normed * student_gain
    d_lifted = d_hidden + scale * (d_unit - unit * jnp.mean(d_unit * unit, axis=-1, keepdims=True))
    grad_embed = f32_dot(rows_f32, d_lifted, TN)[:PIX]

    summed, gain_sum, cosine_sum = sum_everywhere(
        (grad_head, grad_down, grad_up, grad_embed), grad_gain, total
    )
    head_sum, down_sum, up_sum, embed_sum = summed
    mean_distance = 1.0 - cosine_sum / (DEVICES * 2 * BLK)
    return (mean_distance, embed_sum, gain_sum, up_sum, down_sum, head_sum)


def solution(mesh):
    in_specs = (
        P(("student", "pool"), None, None),
        P(("student", "pool"), None),
        P(("student", "pool"), None),
        P(),
        P(),
        P(),
        P(),
        P(),
        P("pool", None, "student"),
        P("pool", None),
        P("pool", None, "student"),
        P("pool", None, "student"),
    )
    out_specs = (P(), P(), P(), P(), P(), P())
    return jax.shard_map(
        on_device, mesh=mesh, in_specs=in_specs, out_specs=out_specs, check_vma=False
    )
```

```python
import jax
import jax.numpy as jnp
from jax import lax
from jax.experimental import pallas as pl
from jax.experimental.pallas import tpu as pltpu
from jax.sharding import PartitionSpec as P

HEADS = 24
HDIM = 64
EPSILON = 1e-06
BOTH = ("student", "pool")
DEVICES = 128
PAIR = 2 * HDIM
LANES = 128
PIX = 588
PIX_PAD = 640
D_S = 384
D_T = 1536
S_HID = 1536
BLK = 128
RANKS = DEVICES // 2
CHUNK = 64
SUM_ROWS = 2 * RANKS * CHUNK
EMBED_ROWS = 592
UP_AT = S_HID
EMBED_AT = UP_AT + D_S * S_HID // LANES
GAIN_AT = EMBED_AT + (D_S // LANES) * EMBED_ROWS
NT = (((1,), (1,)), ((), ()))
TN = (((0,), (0,)), ((), ()))
NN = (((1,), (0,)), ((), ()))


def bf16_dot(left, right, dims):
    return lax.dot_general(left, right, dims, preferred_element_type=jnp.float32)


def rms_scale(values):
    return lax.rsqrt(jnp.mean(values * values, axis=-1, keepdims=True) + EPSILON)


def halved_dot(left, right):
    return (
        bf16_dot(left[0], right[0], NN)
        + bf16_dot(left[1], right[0], NN)
        + bf16_dot(left[0], right[1], NN)
    )


def attention_kernel(mixed_ref, out_ref):
    lane = lax.broadcasted_iota(jnp.int32, (BLK, PAIR), 1)
    first = lane < HDIM
    zero = jnp.zeros((BLK, PAIR), jnp.bfloat16)
    ones = jnp.concatenate(
        [jnp.where(first, 1.0, 0.0), jnp.where(first, 0.0, 1.0)], axis=0
    ).astype(jnp.bfloat16)
    for pair in range(HEADS // 2):
        at = pair * PAIR
        queries = mixed_ref[:, at : at + PAIR]
        keys = mixed_ref[:, D_T + at : D_T + at + PAIR]
        values = mixed_ref[:, 2 * D_T + at : 2 * D_T + at + PAIR]
        keys_two = jnp.concatenate(
            [jnp.where(first, keys, zero), jnp.where(first, zero, keys)], axis=0
        )
        values_two = jnp.concatenate(
            [jnp.where(first, values, zero), jnp.where(first, zero, values)], axis=0
        )
        scores = bf16_dot(queries, keys_two, NT)
        left, right = scores[:, :BLK], scores[:, BLK:]
        scale = HDIM ** (-0.5)
        left = jnp.exp((left - jnp.max(left, axis=1, keepdims=True)) * scale)
        right = jnp.exp((right - jnp.max(right, axis=1, keepdims=True)) * scale)
        weights = jnp.concatenate([left, right], axis=1).astype(jnp.bfloat16)
        summed = bf16_dot(weights, jnp.concatenate([values_two, ones], axis=1), NN)
        out_ref[:, at : at + PAIR] = (summed[:, :PAIR] / summed[:, PAIR:]).astype(jnp.bfloat16)


def attend(mixed):
    rows, total = mixed.shape
    return pl.pallas_call(
        attention_kernel,
        grid=(rows // BLK,),
        in_specs=[pl.BlockSpec((BLK, total), lambda b: (b, 0))],
        out_specs=pl.BlockSpec((BLK, D_T), lambda b: (b, 0)),
        out_shape=jax.ShapeDtypeStruct((rows, D_T), jnp.bfloat16),
        compiler_params=pltpu.CompilerParams(vmem_limit_bytes=32 * 1024 * 1024),
        cost_estimate=pl.CostEstimate(
            flops=rows * BLK * D_T * 8, bytes_accessed=rows * D_T * 8, transcendentals=rows * BLK * HEADS
        ),
        name="attention",
    )(mixed)


def core_groups():
    groups = [[], []]
    for device in range(DEVICES):
        groups[(device // 8) % 2].append(device)
    return groups


def core_swap(values):
    pairs = [(d, d ^ 8) for d in range(DEVICES)]
    return lax.ppermute(values, BOTH, pairs)


def halves_of(values):
    high = lax.reduce_precision(values, 8, 7)
    return high.astype(jnp.bfloat16), (values - high).astype(jnp.bfloat16)


def cut(values):
    high = values.astype(jnp.bfloat16)
    return high, (values - high.astype(jnp.float32)).astype(jnp.bfloat16)


def dot_three(left, right, dims):
    at_left, at_right = dims[0][0][0], dims[0][1][0]
    wide = jnp.concatenate([left[0], left[1], left[0]], axis=at_left)
    other = jnp.concatenate([right[0], right[0], right[1]], axis=at_right)
    return bf16_dot(wide, other, dims)


def scale_of(values):
    return lax.rsqrt(jnp.mean(values * values, axis=1, keepdims=True) + EPSILON)


def head_kernel(
    context, embedded, output, student_out, hidden_hi, hidden_lo, act_hi, act_lo, head_hi, head_lo,
    sums, down_rest, d_hidden_out, total,
):
    @pl.when(pl.program_id(0) == 0)
    def _():
        sums[...] = jnp.zeros_like(sums)
        down_rest[...] = jnp.zeros_like(down_rest)
        total[...] = jnp.zeros_like(total)

    finished = embedded[...] + bf16_dot(context[...], output[...], NT)
    features = (finished * scale_of(finished)).astype(jnp.bfloat16).astype(jnp.float32)
    out = student_out[...]
    dot_mean = jnp.mean(out * features, axis=1, keepdims=True)
    out_scale, feature_scale = scale_of(out), scale_of(features)
    both = out_scale * feature_scale
    total[...] += jnp.sum(dot_mean * both)
    along = both * (-1.0 / D_T)
    back = both * dot_mean * out_scale * out_scale * (1.0 / D_T)
    d_out = cut(along * features + back * out)
    grad_head = dot_three((hidden_hi[...], hidden_lo[...]), d_out, TN)
    for i in range(D_T // LANES):
        sums[i * D_S : (i + 1) * D_S, :] += grad_head[:, i * LANES : (i + 1) * LANES]
    d_hidden = dot_three(d_out, (head_hi[...], head_lo[...]), NT)
    d_hidden_out[...] = d_hidden
    grad_down = dot_three((act_hi[...], act_lo[...]), cut(d_hidden), TN)
    at = D_S * D_T // LANES
    for i in range(2):
        sums[at + i * S_HID : at + (i + 1) * S_HID, :] += grad_down[:, i * LANES : (i + 1) * LANES]
    down_rest[...] += grad_down[:, 2 * LANES :]


def head_backward(context, embedded, output, student_out, hidden, act, head):
    rows = context.shape[0]
    block = 256

    def by_row(columns):
        return pl.BlockSpec((block, columns), lambda r: (r, 0))

    def whole(shape):
        return pl.BlockSpec(shape, lambda r: (0, 0))

    return pl.pallas_call(
        head_kernel,
        grid=(rows // block,),
        in_specs=[
            by_row(D_T), by_row(D_T), whole((D_T, D_T)), by_row(D_T), by_row(D_S), by_row(D_S),
            by_row(S_HID), by_row(S_HID), whole((D_S, D_T)), whole((D_S, D_T)),
        ],
        out_specs=[whole((SUM_ROWS, LANES)), whole((S_HID, LANES)), by_row(D_S), whole((8, LANES))],
        out_shape=[
            jax.ShapeDtypeStruct((SUM_ROWS, LANES), jnp.float32),
            jax.ShapeDtypeStruct((S_HID, LANES), jnp.float32),
            jax.ShapeDtypeStruct((rows, D_S), jnp.float32),
            jax.ShapeDtypeStruct((8, LANES), jnp.float32),
        ],
        compiler_params=pltpu.CompilerParams(vmem_limit_bytes=56 * 1024 * 1024),
        cost_estimate=pl.CostEstimate(
            flops=2 * rows * D_T * (D_T + 9 * D_S), bytes_accessed=40 * 1024 * 1024, transcendentals=0
        ),
        name="head_backward",
    )(context, embedded, output, student_out, *hidden, *act, *head)


def trunk_kernel(
    d_hidden, slope, down_hi, down_lo, up_hi, up_lo, normed_hi, normed_lo, unit, scale, gain, rows,
    down_rest, total, sums, dh_hi, dh_lo, d_normed,
):
    step = pl.program_id(0)
    tile = slope.shape[1]

    @pl.when(step == 0)
    def _():
        dh_hi[...], dh_lo[...] = cut(d_hidden[...])
        d_normed[...] = jnp.zeros_like(d_normed)
        sums[:UP_AT, :] = down_rest[...]
        sums[GAIN_AT:, :] = jnp.zeros((SUM_ROWS - GAIN_AT, LANES), jnp.float32)

    d_act = dot_three((dh_hi[...], dh_lo[...]), (down_hi[...], down_lo[...]), NT)
    d_pre = cut(d_act * slope[...])
    grad_up = dot_three((normed_hi[...], normed_lo[...]), d_pre, TN)
    at = pl.multiple_of(UP_AT + step * (tile // LANES) * D_S, LANES)
    for i in range(tile // LANES):
        sums[pl.ds(at + i * D_S, D_S), :] = grad_up[:, i * LANES : (i + 1) * LANES]
    d_normed[...] += dot_three(d_pre, (up_hi[...], up_lo[...]), NT)

    @pl.when(step == pl.num_programs(0) - 1)
    def _():
        d_out = d_normed[...]
        across = unit[...]
        grad_gain = jnp.sum(d_out * across, axis=0, keepdims=True)
        d_unit = d_out * gain[...]
        inner = jnp.mean(d_unit * across, axis=1, keepdims=True)
        d_lifted = cut(d_hidden[...] + scale[...] * (d_unit - across * inner))
        grad_embed = bf16_dot(rows[...], d_lifted[0], TN) + bf16_dot(rows[...], d_lifted[1], TN)
        for i in range(D_S // LANES):
            columns = slice(i * LANES, (i + 1) * LANES)
            start = EMBED_AT + i * EMBED_ROWS
            sums[start : start + EMBED_ROWS, :] = grad_embed[:EMBED_ROWS, columns]
            sums[GAIN_AT + i : GAIN_AT + i + 1, :] = grad_gain[:, columns]
        first, rest = cut(total[0:1, :])
        first = first.astype(jnp.float32)
        second, third = cut(total[0:1, :] - first)
        lane = lax.broadcasted_iota(jnp.int32, (1, LANES), 1)
        row = jnp.where(
            lane == 0,
            first,
            jnp.where(lane == 1, second.astype(jnp.float32), third.astype(jnp.float32)),
        )
        sums[SUM_ROWS - 1 :, :] = jnp.where(lane < 3, row, 0.0)


def trunk_backward(d_hidden, slope, down, up, normed, unit, scale, gain, rows, down_rest, total):
    count = d_hidden.shape[0]
    tile = 256

    def whole(values):
        return pl.BlockSpec(values.shape, lambda j: (0, 0))

    down_spec = pl.BlockSpec((tile, D_S), lambda j: (j, 0))
    up_spec = pl.BlockSpec((D_S, tile), lambda j: (0, j))
    return pl.pallas_call(
        trunk_kernel,
        grid=(S_HID // tile,),
        in_specs=[
            whole(d_hidden), pl.BlockSpec((count, tile), lambda j: (0, j)),
            down_spec, down_spec, up_spec, up_spec,
            whole(normed[0]), whole(normed[1]), whole(unit), whole(scale), whole(gain), whole(rows),
            whole(down_rest), whole(total),
        ],
        out_specs=pl.BlockSpec((SUM_ROWS, LANES), lambda j: (0, 0)),
        out_shape=jax.ShapeDtypeStruct((SUM_ROWS, LANES), jnp.float32),
        scratch_shapes=[
            pltpu.VMEM((count, D_S), jnp.bfloat16),
            pltpu.VMEM((count, D_S), jnp.bfloat16),
            pltpu.VMEM((count, D_S), jnp.float32),
        ],
        compiler_params=pltpu.CompilerParams(vmem_limit_bytes=56 * 1024 * 1024),
        cost_estimate=pl.CostEstimate(
            flops=2 * count * D_S * (9 * S_HID + 2 * PIX_PAD), bytes_accessed=30 * 1024 * 1024, transcendentals=0
        ),
        name="trunk_backward",
    )(d_hidden, slope, *down, *up, *normed, unit, scale, gain, rows, down_rest, total)


def unpack_kernel(core, a_mine, a_theirs, b_mine, b_theirs, head, down, up, embed, gain, total):
    def unpack(a_low, a_high, b_low, b_high):
        half = SUM_ROWS // 2

        def take(low, high, start, count):
            stop = start + count
            parts = []
            if start < half:
                parts.append(low[start : min(stop, half), :])
            if stop > half:
                parts.append(high[max(start, half) - half : stop - half, :])
            parts = [part.astype(jnp.float32) for part in parts]
            return parts[0] if len(parts) == 1 else jnp.concatenate(parts, axis=0)

        for i in range(D_T // LANES):
            columns = slice(i * LANES, (i + 1) * LANES)
            head[:, columns] = take(a_low, a_high, i * D_S, D_S)
            up[:, columns] = take(b_low, b_high, UP_AT + i * D_S, D_S)
        at = D_S * D_T // LANES
        for i in range(2):
            down[:, i * LANES : (i + 1) * LANES] = take(a_low, a_high, at + i * S_HID, S_HID)
        down[:, 2 * LANES :] = take(b_low, b_high, 0, S_HID)
        for i in range(D_S // LANES):
            columns = slice(i * LANES, (i + 1) * LANES)
            embed[:, columns] = take(b_low, b_high, EMBED_AT + i * EMBED_ROWS, EMBED_ROWS)[:PIX]
        gain[...] = take(b_low, b_high, GAIN_AT, 16)[:8]
        total[...] = take(b_low, b_high, SUM_ROWS - 16, 16)[8:]

    @pl.when(core[0] == 0)
    def _():
        unpack(a_mine, a_theirs, b_mine, b_theirs)

    @pl.when(core[0] == 1)
    def _():
        unpack(a_theirs, a_mine, b_theirs, b_mine)


def unpack_sums(core, a_mine, a_theirs, b_mine, b_theirs):
    vmem = pl.BlockSpec(memory_space=pltpu.VMEM)
    shapes = [(D_S, D_T), (S_HID, D_S), (D_S, S_HID), (PIX, D_S), (8, LANES), (8, LANES)]
    return pl.pallas_call(
        unpack_kernel,
        in_specs=[pl.BlockSpec(memory_space=pltpu.SMEM)] + [vmem] * 4,
        out_specs=[vmem] * 6,
        out_shape=[jax.ShapeDtypeStruct(shape, jnp.float32) for shape in shapes],
        compiler_params=pltpu.CompilerParams(vmem_limit_bytes=56 * 1024 * 1024),
        cost_estimate=pl.CostEstimate(flops=0, bytes_accessed=12 * 1024 * 1024, transcendentals=0),
        name="unpack_sums",
    )(core.reshape(1), a_mine, a_theirs, b_mine, b_theirs)


def scatter_sum(sums, core):
    halves = sums.reshape(2, SUM_ROWS // 2, LANES)
    mine = lax.dynamic_index_in_dim(halves, core, 0, keepdims=False)
    other = lax.dynamic_index_in_dim(halves, 1 - core, 0, keepdims=False)
    mine = mine + core_swap(other)
    sent = mine.astype(jnp.bfloat16).reshape(RANKS, CHUNK, LANES)
    got = lax.all_to_all(sent, BOTH, 0, 0, axis_index_groups=core_groups(), tiled=True)
    return jnp.sum(got.astype(jnp.float32), axis=0)


def spread_chunk(chunk):
    spread = jnp.broadcast_to(chunk.astype(jnp.bfloat16)[None], (RANKS, CHUNK, LANES))
    half = lax.all_to_all(spread, BOTH, 0, 0, axis_index_groups=core_groups(), tiled=True)
    half = half.reshape(SUM_ROWS // 2, LANES)
    return half, core_swap(half)


def keep_total(chunk, core):
    rank = (lax.axis_index("student") // 2) * 8 + lax.axis_index("pool")
    owner = jnp.logical_and(core == 1, rank == RANKS - 1)
    whole = jnp.sum(chunk[CHUNK - 1, :3])
    first = lax.reduce_precision(whole, 8, 7)
    second = lax.reduce_precision(whole - first, 8, 7)
    lane = lax.broadcasted_iota(jnp.int32, (CHUNK, LANES), 1)
    row = jnp.where(lane == 0, first, jnp.where(lane == 1, second, whole - first - second))
    last = lax.broadcasted_iota(jnp.int32, (CHUNK, LANES), 0) == CHUNK - 1
    return jnp.where(jnp.logical_and(owner, last), row, chunk)


def on_device(
    pixels,
    keyframes,
    destination,
    student_embed,
    student_gain,
    student_up,
    student_down,
    student_head,
    teacher_embed,
    teacher_gain,
    teacher_project,
    teacher_output,
):
    pool_size = lax.axis_size("pool")

    def gathered(shard):
        return lax.all_gather(shard, "student", axis=0, tiled=True)

    embed_full = gathered(jnp.pad(teacher_embed[0].T, ((0, 0), (0, PIX_PAD - PIX))))
    project_full = gathered(teacher_project[0].T)
    output_full = gathered(teacher_output[0].T)

    teachers = jnp.arange(pool_size, dtype=jnp.int32)[:, None, None]
    chosen = [
        lax.dynamic_index_in_dim(pixels, keyframes[0, k], 0, keepdims=True) for k in range(2)
    ]
    outgoing = jnp.where(
        destination[0, 0] == teachers,
        chosen[0],
        jnp.where(destination[0, 1] == teachers, chosen[1], jnp.zeros((), jnp.bfloat16)),
    )
    outgoing = jnp.pad(outgoing, ((0, 0), (0, 0), (0, PIX_PAD - PIX)))
    arrived = lax.all_to_all(outgoing, "pool", split_axis=0, concat_axis=0, tiled=True)
    rows = arrived.reshape(pool_size * BLK, PIX_PAD)

    embed = jnp.pad(student_embed, ((0, PIX_PAD - PIX), (0, 0)))
    embed = halves_of(embed)
    lifted = bf16_dot(rows, embed[0], NN) + bf16_dot(rows, embed[1], NN)
    scale = rms_scale(lifted)
    unit = lifted * scale
    normed_s = halves_of(unit * student_gain)
    up = halves_of(student_up)
    down = halves_of(student_down)
    head = halves_of(student_head)
    pre = halved_dot(normed_s, up)
    cdf = 0.5 * (1.0 + lax.erf(pre * (2.0**-0.5)))
    act = halves_of(pre * cdf)
    slope = cdf + pre * jnp.exp(-0.5 * pre * pre) * ((2.0 * jnp.pi) ** -0.5)
    hidden = halves_of(lifted + halved_dot(act, down))
    student_out = halved_dot(hidden, head)

    embedded = bf16_dot(rows, embed_full, NT)
    normed = (embedded * rms_scale(embedded) * teacher_gain[0]).astype(jnp.bfloat16)
    mixed = bf16_dot(normed, project_full, NT).astype(jnp.bfloat16)
    context = attend(mixed)

    core = lax.rem(lax.axis_index("student"), 2)
    sums_a, down_rest, d_hidden, total = head_backward(
        context, embedded, output_full, student_out, hidden, act, head
    )
    chunk_a = scatter_sum(sums_a, core)
    sums_b = trunk_backward(
        d_hidden, slope, down, up, normed_s, unit, scale, student_gain[None], rows, down_rest, total
    )
    chunk_b = keep_total(scatter_sum(sums_b, core), core)
    head_sum, down_sum, up_sum, embed_sum, gain_sum, cosine_sum = unpack_sums(
        core, *spread_chunk(chunk_a), *spread_chunk(chunk_b)
    )
    gain_sum = gain_sum[: D_S // LANES].reshape(D_S)
    mean_distance = 1.0 - jnp.sum(cosine_sum[7, :3]) / (DEVICES * 2 * BLK)
    return (mean_distance, embed_sum, gain_sum, up_sum, down_sum, head_sum)


def solution(mesh):
    in_specs = (
        P(("student", "pool"), None, None),
        P(("student", "pool"), None),
        P(("student", "pool"), None),
        P(),
        P(),
        P(),
        P(),
        P(),
        P("pool", None, "student"),
        P("pool", None),
        P("pool", None, "student"),
        P("pool", None, "student"),
    )
    out_specs = (P(), P(), P(), P(), P(), P())
    return jax.shard_map(
        on_device, mesh=mesh, in_specs=in_specs, out_specs=out_specs, check_vma=False
    )
```

```python
import jax
import jax.numpy as jnp
from jax import lax
from jax.experimental import pallas as pl
from jax.experimental.pallas import tpu as pltpu
from jax.sharding import PartitionSpec as P

HEADS = 24
HDIM = 64
EPSILON = 1e-06
BOTH = ("student", "pool")
DEVICES = 128
PAIR = 2 * HDIM
LANES = 128
PIX = 588
PIX_PAD = 640
D_S = 384
D_T = 1536
S_HID = 1536
BLK = 128
P_ROWS = 288
O_ROWS = 96
NEAR = 12
FAR = 4
CUT = 192
REST = P_ROWS - CUT
STUDENTS = 16
EMBED_PACK = 48
RANKS = DEVICES // 2
CHUNK = 64
SUM_ROWS = 2 * RANKS * CHUNK
EMBED_ROWS = 592
UP_AT = S_HID
EMBED_AT = UP_AT + D_S * S_HID // LANES
GAIN_AT = EMBED_AT + (D_S // LANES) * EMBED_ROWS
NT = (((1,), (1,)), ((), ()))
TN = (((0,), (0,)), ((), ()))
NN = (((1,), (0,)), ((), ()))


def bf16_dot(left, right, dims):
    return lax.dot_general(left, right, dims, preferred_element_type=jnp.float32)


def rms_scale(values):
    return lax.rsqrt(jnp.mean(values * values, axis=-1, keepdims=True) + EPSILON)


def halved_dot(left, right):
    return (
        bf16_dot(left[0], right[0], NN)
        + bf16_dot(left[1], right[0], NN)
        + bf16_dot(left[0], right[1], NN)
    )


def attend_block(mixed, at, out, base):
    lane = lax.broadcasted_iota(jnp.int32, (BLK, PAIR), 1)
    first = lane < HDIM
    zero = jnp.zeros((BLK, PAIR), jnp.bfloat16)
    ones = jnp.concatenate(
        [jnp.where(first, 1.0, 0.0), jnp.where(first, 0.0, 1.0)], axis=0
    ).astype(jnp.bfloat16)
    rows = pl.ds(at, BLK)
    for pair in range(HEADS // 2):
        start = pair * PAIR
        queries = mixed[rows, start : start + PAIR]
        keys = mixed[rows, D_T + start : D_T + start + PAIR]
        values = mixed[rows, 2 * D_T + start : 2 * D_T + start + PAIR]
        keys_two = jnp.concatenate(
            [jnp.where(first, keys, zero), jnp.where(first, zero, keys)], axis=0
        )
        values_two = jnp.concatenate(
            [jnp.where(first, values, zero), jnp.where(first, zero, values)], axis=0
        )
        scores = bf16_dot(queries, keys_two, NT)
        left, right = scores[:, :BLK], scores[:, BLK:]
        scale = HDIM ** (-0.5)
        left = jnp.exp((left - jnp.max(left, axis=1, keepdims=True)) * scale)
        right = jnp.exp((right - jnp.max(right, axis=1, keepdims=True)) * scale)
        weights = jnp.concatenate([left, right], axis=1).astype(jnp.bfloat16)
        summed = bf16_dot(weights, jnp.concatenate([values_two, ones], axis=1), NN)
        out[rows, start : start + PAIR] = (summed[:, :PAIR] / summed[:, PAIR:]).astype(jnp.bfloat16)


def shard_copies(plan, owners, target, semaphores, count):
    copies = []
    for i, (piece, start, rows, row) in enumerate(plan):
        at = pl.multiple_of(owners[i] * count + row, 16)
        copies.append(
            pltpu.make_async_copy(
                piece.at[pl.ds(start, rows)], target.at[pl.ds(at, rows)], semaphores.at[i]
            )
        )
    return copies


def teacher_kernel(owners, rows, gain, gathered, *rest):
    pieces, rest = rest[: NEAR + FAR], rest[NEAR + FAR :]
    embedded, context, embed, project, normed, mixed, semaphores, others = rest
    wide = D_T // 2
    first = [
        pltpu.make_async_copy(
            gathered.at[:, pl.ds(CUT, EMBED_PACK), pl.ds(i * wide, wide)], embed.at[:, i], others.at[i]
        )
        for i in range(2)
    ]
    for copy in first:
        copy.start()
    copies = [
        pltpu.make_async_copy(
            gathered.at[i, pl.ds(0, CUT)], project.at[pl.ds(i * P_ROWS, CUT)], others.at[2 + i]
        )
        for i in range(STUDENTS)
    ]
    plan = [(piece, 0, P_ROWS - CUT, CUT) for piece in pieces]
    copies += shard_copies(plan, owners, project, semaphores, P_ROWS)
    for copy in copies:
        copy.start()
    for copy in first:
        copy.wait()
    step = 2 * BLK

    @pl.loop(0, rows.shape[0] // step)
    def _(r):
        at = pl.ds(pl.multiple_of(r * step, step), step)
        weights = embed[...].reshape(D_T, wide)[:, :PIX_PAD]
        product = bf16_dot(rows[at, :], weights, NT)
        embedded[at, :] = product
        normed[at, :] = (product * scale_of(product) * gain[...]).astype(jnp.bfloat16)

    for copy in copies:
        copy.wait()
    tile = 512

    @pl.loop(0, 3 * D_T // tile)
    def _(n):
        at = pl.ds(pl.multiple_of(n * tile, tile), tile)
        mixed[:, at] = bf16_dot(normed[...], project[at, :], NT).astype(jnp.bfloat16)

    @pl.loop(0, rows.shape[0] // BLK)
    def _(b):
        at = pl.multiple_of(b * BLK, BLK)
        attend_block(mixed, at, context, at)


def teach(owners, rows, gain, gathered, pieces):
    count = rows.shape[0]
    vmem = pl.BlockSpec(memory_space=pltpu.VMEM)
    return pl.pallas_call(
        teacher_kernel,
        in_specs=[pl.BlockSpec(memory_space=pltpu.SMEM)] + [vmem] * 2
        + [pl.BlockSpec(memory_space=pl.ANY)] * (1 + NEAR + FAR),
        out_specs=[vmem] * 2,
        out_shape=[
            jax.ShapeDtypeStruct((count, D_T), jnp.float32),
            jax.ShapeDtypeStruct((count, D_T), jnp.bfloat16),
        ],
        scratch_shapes=[
            pltpu.VMEM((STUDENTS, 2, EMBED_PACK, D_T // 2), jnp.bfloat16),
            pltpu.VMEM((3 * D_T, D_T), jnp.bfloat16),
            pltpu.VMEM((count, D_T), jnp.bfloat16),
            pltpu.VMEM((count, 3 * D_T), jnp.bfloat16),
            pltpu.SemaphoreType.DMA((NEAR + FAR,)),
            pltpu.SemaphoreType.DMA((2 + STUDENTS,)),
        ],
        compiler_params=pltpu.CompilerParams(vmem_limit_bytes=58 * 1024 * 1024),
        cost_estimate=pl.CostEstimate(
            flops=2 * count * D_T * (PIX_PAD + 3 * D_T), bytes_accessed=30 * 1024 * 1024, transcendentals=0
        ),
        name="teacher",
    )(owners, rows, gain, gathered, *pieces)


def place(device):
    student, pool = device // 8, device % 8
    return [student // 4, student // 2 % 2, student % 2, pool]


def moved(values, x=0, z=0, core=0):
    pairs = []
    for device in range(DEVICES):
        at = place(device)
        student = ((at[0] + x) % 4 * 2 + (at[1] ^ z)) * 2 + (at[2] ^ core)
        pairs.append((device, student * 8 + at[3]))
    return lax.ppermute(values, BOTH, pairs)


def with_core(pieces):
    return pieces + [moved(values, core=1) for values in pieces]


def shard_owners():
    x, z, core, _ = place(lax.axis_index("student") * 8)

    def index(dx, dz, dc):
        return (lax.rem(x + dx + 4, 4) * 2 + (z + dz) % 2) * 2 + (core + dc) % 2

    near = [index(dx, dz, dc) for dc in range(2) for dx in (0, -1, 1) for dz in range(2)]
    far = [index(2, dz, dc) for dc in range(2) for dz in range(2)]
    return jnp.stack(near + far).astype(jnp.int32)


def core_groups():
    groups = [[], []]
    for device in range(DEVICES):
        groups[(device // 8) % 2].append(device)
    return groups


def core_swap(values):
    pairs = [(d, d ^ 8) for d in range(DEVICES)]
    return lax.ppermute(values, BOTH, pairs)


def halves_of(values):
    high = lax.reduce_precision(values, 8, 7)
    return high.astype(jnp.bfloat16), (values - high).astype(jnp.bfloat16)


def cut(values):
    high = values.astype(jnp.bfloat16)
    return high, (values - high.astype(jnp.float32)).astype(jnp.bfloat16)


def dot_three(left, right, dims):
    at_left, at_right = dims[0][0][0], dims[0][1][0]
    wide = jnp.concatenate([left[0], left[1], left[0]], axis=at_left)
    other = jnp.concatenate([right[0], right[0], right[1]], axis=at_right)
    return bf16_dot(wide, other, dims)


def scale_of(values):
    return lax.rsqrt(jnp.mean(values * values, axis=1, keepdims=True) + EPSILON)


def hand_over(core, sums, mine, other, done):
    half = SUM_ROWS // 2
    at = pl.multiple_of(core * half, half)
    across = pl.multiple_of((1 - core) * half, half)
    copies = [
        pltpu.make_async_copy(sums.at[pl.ds(across, half)], other, done.at[0]),
        pltpu.make_async_copy(sums.at[pl.ds(at, half)], mine, done.at[1]),
    ]
    for copy in copies:
        copy.start()
    for copy in copies:
        copy.wait()


def head_kernel(
    core, owners, context, embedded, student_out, hidden_hi, hidden_lo, act_hi, act_lo, head_hi, head_lo,
    *rest,
):
    pieces, rest = rest[: NEAR + FAR], rest[NEAR + FAR :]
    mine, other, down_rest, d_hidden_out, total, sums, output, semaphores, done = rest

    @pl.when(pl.program_id(0) == 0)
    def _():
        plan = [(piece, REST if i < NEAR else 0, O_ROWS, 0) for i, piece in enumerate(pieces)]
        copies = shard_copies(plan, owners, output, semaphores, O_ROWS)
        for copy in copies:
            copy.start()
        for copy in copies:
            copy.wait()
        sums[...] = jnp.zeros_like(sums)
        down_rest[...] = jnp.zeros_like(down_rest)
        total[...] = jnp.zeros_like(total)

    finished = embedded[...] + bf16_dot(context[...], output[...], NT)
    features = (finished * scale_of(finished)).astype(jnp.bfloat16).astype(jnp.float32)
    out = student_out[...]
    dot_mean = jnp.mean(out * features, axis=1, keepdims=True)
    out_scale, feature_scale = scale_of(out), scale_of(features)
    both = out_scale * feature_scale
    total[...] += jnp.sum(dot_mean * both)
    along = both * (-1.0 / D_T)
    back = both * dot_mean * out_scale * out_scale * (1.0 / D_T)
    d_out = cut(along * features + back * out)
    grad_head = dot_three((hidden_hi[...], hidden_lo[...]), d_out, TN)
    for i in range(D_T // LANES):
        sums[i * D_S : (i + 1) * D_S, :] += grad_head[:, i * LANES : (i + 1) * LANES]
    d_hidden = dot_three(d_out, (head_hi[...], head_lo[...]), NT)
    d_hidden_out[...] = d_hidden
    grad_down = dot_three((act_hi[...], act_lo[...]), cut(d_hidden), TN)
    at = D_S * D_T // LANES
    for i in range(2):
        sums[at + i * S_HID : at + (i + 1) * S_HID, :] += grad_down[:, i * LANES : (i + 1) * LANES]
    down_rest[...] += grad_down[:, 2 * LANES :]

    @pl.when(pl.program_id(0) == pl.num_programs(0) - 1)
    def _():
        hand_over(core[0], sums, mine, other, done)


def head_backward(core, owners, context, embedded, student_out, hidden, act, head, pieces):
    rows = context.shape[0]
    block = 256

    def by_row(columns):
        return pl.BlockSpec((block, columns), lambda r: (r, 0))

    def whole(shape):
        return pl.BlockSpec(shape, lambda r: (0, 0))

    return pl.pallas_call(
        head_kernel,
        grid=(rows // block,),
        in_specs=[
            pl.BlockSpec(memory_space=pltpu.SMEM),
            pl.BlockSpec(memory_space=pltpu.SMEM),
            by_row(D_T), by_row(D_T), by_row(D_T), by_row(D_S), by_row(D_S),
            by_row(S_HID), by_row(S_HID), whole((D_S, D_T)), whole((D_S, D_T)),
        ]
        + [pl.BlockSpec(memory_space=pl.ANY)] * (NEAR + FAR),
        out_specs=[pl.BlockSpec(memory_space=pl.ANY)] * 2
        + [whole((S_HID, LANES)), by_row(D_S), whole((8, LANES))],
        out_shape=[
            jax.ShapeDtypeStruct((SUM_ROWS // 2, LANES), jnp.float32),
            jax.ShapeDtypeStruct((SUM_ROWS // 2, LANES), jnp.float32),
            jax.ShapeDtypeStruct((S_HID, LANES), jnp.float32),
            jax.ShapeDtypeStruct((rows, D_S), jnp.float32),
            jax.ShapeDtypeStruct((8, LANES), jnp.float32),
        ],
        scratch_shapes=[
            pltpu.VMEM((SUM_ROWS, LANES), jnp.float32),
            pltpu.VMEM((D_T, D_T), jnp.bfloat16),
            pltpu.SemaphoreType.DMA((NEAR + FAR,)),
            pltpu.SemaphoreType.DMA((2,)),
        ],
        compiler_params=pltpu.CompilerParams(vmem_limit_bytes=56 * 1024 * 1024),
        cost_estimate=pl.CostEstimate(
            flops=2 * rows * D_T * (D_T + 9 * D_S), bytes_accessed=40 * 1024 * 1024, transcendentals=0
        ),
        name="head_backward",
    )(core, owners, context, embedded, student_out, *hidden, *act, *head, *pieces)


def trunk_kernel(
    core, d_hidden, slope, down_hi, down_lo, up_hi, up_lo, normed_hi, normed_lo, unit, scale, gain, rows,
    down_rest, total, mine, other, sums, dh_hi, dh_lo, d_normed, done,
):
    step = pl.program_id(0)
    tile = slope.shape[1]

    @pl.when(step == 0)
    def _():
        dh_hi[...], dh_lo[...] = cut(d_hidden[...])
        d_normed[...] = jnp.zeros_like(d_normed)
        sums[:UP_AT, :] = down_rest[...]
        sums[GAIN_AT:, :] = jnp.zeros((SUM_ROWS - GAIN_AT, LANES), jnp.float32)

    d_act = dot_three((dh_hi[...], dh_lo[...]), (down_hi[...], down_lo[...]), NT)
    d_pre = cut(d_act * slope[...])
    grad_up = dot_three((normed_hi[...], normed_lo[...]), d_pre, TN)
    at = pl.multiple_of(UP_AT + step * (tile // LANES) * D_S, LANES)
    for i in range(tile // LANES):
        sums[pl.ds(at + i * D_S, D_S), :] = grad_up[:, i * LANES : (i + 1) * LANES]
    d_normed[...] += dot_three(d_pre, (up_hi[...], up_lo[...]), NT)

    @pl.when(step == pl.num_programs(0) - 1)
    def _():
        d_out = d_normed[...]
        across = unit[...]
        grad_gain = jnp.sum(d_out * across, axis=0, keepdims=True)
        d_unit = d_out * gain[...]
        inner = jnp.mean(d_unit * across, axis=1, keepdims=True)
        d_lifted = cut(d_hidden[...] + scale[...] * (d_unit - across * inner))
        grad_embed = bf16_dot(rows[...], d_lifted[0], TN) + bf16_dot(rows[...], d_lifted[1], TN)
        for i in range(D_S // LANES):
            columns = slice(i * LANES, (i + 1) * LANES)
            start = EMBED_AT + i * EMBED_ROWS
            sums[start : start + EMBED_ROWS, :] = grad_embed[:EMBED_ROWS, columns]
            sums[GAIN_AT + i : GAIN_AT + i + 1, :] = grad_gain[:, columns]
        first, rest = cut(total[0:1, :])
        first = first.astype(jnp.float32)
        second, third = cut(total[0:1, :] - first)
        lane = lax.broadcasted_iota(jnp.int32, (1, LANES), 1)
        row = jnp.where(
            lane == 0,
            first,
            jnp.where(lane == 1, second.astype(jnp.float32), third.astype(jnp.float32)),
        )
        sums[SUM_ROWS - 1 :, :] = jnp.where(lane < 3, row, 0.0)
        hand_over(core[0], sums, mine, other, done)


def trunk_backward(core, d_hidden, slope, down, up, normed, unit, scale, gain, rows, down_rest, total):
    count = d_hidden.shape[0]
    tile = 256

    def whole(values):
        return pl.BlockSpec(values.shape, lambda j: (0, 0))

    down_spec = pl.BlockSpec((tile, D_S), lambda j: (j, 0))
    up_spec = pl.BlockSpec((D_S, tile), lambda j: (0, j))
    return pl.pallas_call(
        trunk_kernel,
        grid=(S_HID // tile,),
        in_specs=[
            pl.BlockSpec(memory_space=pltpu.SMEM),
            whole(d_hidden), pl.BlockSpec((count, tile), lambda j: (0, j)),
            down_spec, down_spec, up_spec, up_spec,
            whole(normed[0]), whole(normed[1]), whole(unit), whole(scale), whole(gain), whole(rows),
            whole(down_rest), whole(total),
        ],
        out_specs=[pl.BlockSpec(memory_space=pl.ANY)] * 2,
        out_shape=[jax.ShapeDtypeStruct((SUM_ROWS // 2, LANES), jnp.float32)] * 2,
        scratch_shapes=[
            pltpu.VMEM((SUM_ROWS, LANES), jnp.float32),
            pltpu.VMEM((count, D_S), jnp.bfloat16),
            pltpu.VMEM((count, D_S), jnp.bfloat16),
            pltpu.VMEM((count, D_S), jnp.float32),
            pltpu.SemaphoreType.DMA((2,)),
        ],
        compiler_params=pltpu.CompilerParams(vmem_limit_bytes=56 * 1024 * 1024),
        cost_estimate=pl.CostEstimate(
            flops=2 * count * D_S * (9 * S_HID + 2 * PIX_PAD), bytes_accessed=30 * 1024 * 1024, transcendentals=0
        ),
        name="trunk_backward",
    )(core, d_hidden, slope, *down, *up, *normed, unit, scale, gain, rows, down_rest, total)


def unpack_kernel(core, mine, theirs, head, down, up, embed, gain, total):
    def unpack(low, high):
        def take(part, start, count):
            pieces, stop = [], start + count
            while start < stop:
                rank, row = start // CHUNK, start % CHUNK
                ref = low if rank < RANKS else high
                size = min(CHUNK - row, stop - start)
                at = part * CHUNK + row
                pieces.append(ref[rank % RANKS, at : at + size, :].astype(jnp.float32))
                start += size
            return pieces[0] if len(pieces) == 1 else jnp.concatenate(pieces, axis=0)

        for i in range(D_T // LANES):
            columns = slice(i * LANES, (i + 1) * LANES)
            head[:, columns] = take(0, i * D_S, D_S)
            up[:, columns] = take(1, UP_AT + i * D_S, D_S)
        at = D_S * D_T // LANES
        for i in range(2):
            down[:, i * LANES : (i + 1) * LANES] = take(0, at + i * S_HID, S_HID)
        down[:, 2 * LANES :] = take(1, 0, S_HID)
        for i in range(D_S // LANES):
            columns = slice(i * LANES, (i + 1) * LANES)
            embed[:, columns] = take(1, EMBED_AT + i * EMBED_ROWS, EMBED_ROWS)[:PIX]
        gain[...] = take(1, GAIN_AT, 16)[:8]
        total[...] = take(1, SUM_ROWS - 16, 16)[8:]

    @pl.when(core[0] == 0)
    def _():
        unpack(mine, theirs)

    @pl.when(core[0] == 1)
    def _():
        unpack(theirs, mine)


def unpack_sums(core, mine, theirs):
    vmem = pl.BlockSpec(memory_space=pltpu.VMEM)
    shapes = [(D_S, D_T), (S_HID, D_S), (D_S, S_HID), (PIX, D_S), (8, LANES), (8, LANES)]
    return pl.pallas_call(
        unpack_kernel,
        in_specs=[pl.BlockSpec(memory_space=pltpu.SMEM)] + [vmem] * 2,
        out_specs=[vmem] * 6,
        out_shape=[jax.ShapeDtypeStruct(shape, jnp.float32) for shape in shapes],
        compiler_params=pltpu.CompilerParams(vmem_limit_bytes=56 * 1024 * 1024),
        cost_estimate=pl.CostEstimate(flops=0, bytes_accessed=12 * 1024 * 1024, transcendentals=0),
        name="unpack_sums",
    )(core, mine, theirs)


def core_sum(mine, other):
    return (mine + core_swap(other)).astype(jnp.bfloat16).reshape(RANKS, CHUNK, LANES)


def chunk_sum(sent):
    got = lax.all_to_all(sent, BOTH, 0, 0, axis_index_groups=core_groups(), tiled=True)
    return jnp.sum(got.astype(jnp.float32), axis=0)


def spread_chunk(chunk):
    spread = jnp.broadcast_to(chunk[None], (RANKS,) + chunk.shape)
    half = lax.all_to_all(spread, BOTH, 0, 0, axis_index_groups=core_groups(), tiled=True)
    return half, core_swap(half)


def keep_total(chunk, core):
    rank = (lax.axis_index("student") // 2) * 8 + lax.axis_index("pool")
    owner = jnp.logical_and(core == 1, rank == RANKS - 1)
    whole = jnp.sum(chunk[CHUNK - 1, :3])
    first = lax.reduce_precision(whole, 8, 7)
    second = lax.reduce_precision(whole - first, 8, 7)
    lane = lax.broadcasted_iota(jnp.int32, (CHUNK, LANES), 1)
    row = jnp.where(lane == 0, first, jnp.where(lane == 1, second, whole - first - second))
    last = lax.broadcasted_iota(jnp.int32, (CHUNK, LANES), 0) == CHUNK - 1
    return jnp.where(jnp.logical_and(owner, last), row, chunk)


def on_device(
    pixels,
    keyframes,
    destination,
    student_embed,
    student_gain,
    student_up,
    student_down,
    student_head,
    teacher_embed,
    teacher_gain,
    teacher_project,
    teacher_output,
):
    pool_size = lax.axis_size("pool")

    project = teacher_project[0].T
    embed_shard = jnp.pad(teacher_embed[0].T, ((0, 0), (0, D_T // 2 - PIX)))
    embed_shard = jnp.concatenate([embed_shard[:EMBED_PACK], embed_shard[EMBED_PACK:]], axis=1)
    gathered = lax.all_gather(
        jnp.concatenate([project[:CUT], embed_shard], axis=0), "student", axis=0, tiled=False
    )
    shard = jnp.concatenate([project[CUT:], teacher_output[0].T], axis=0)
    first = [moved(shard, z=1), moved(shard, x=1), moved(shard, x=-1)]

    owners = shard_owners()

    teachers = jnp.arange(pool_size, dtype=jnp.int32)[:, None, None]
    chosen = [
        lax.dynamic_index_in_dim(pixels, keyframes[0, k], 0, keepdims=True) for k in range(2)
    ]
    outgoing = jnp.where(
        destination[0, 0] == teachers,
        chosen[0],
        jnp.where(destination[0, 1] == teachers, chosen[1], jnp.zeros((), jnp.bfloat16)),
    )
    outgoing = jnp.pad(outgoing, ((0, 0), (0, 0), (0, PIX_PAD - PIX)))
    up, down, head = halves_of(student_up), halves_of(student_down), halves_of(student_head)
    embed = halves_of(jnp.pad(student_embed, ((0, PIX_PAD - PIX), (0, 0))))
    outgoing, up, down, head, embed, *first = lax.optimization_barrier(
        (outgoing, up, down, head, embed, *first)
    )
    across, back, ahead = first
    second = [
        moved(across, x=1), moved(across, x=-1), moved(back[:REST], x=1), moved(ahead[REST:], x=-1)
    ]
    arrived = lax.all_to_all(outgoing, "pool", split_axis=0, concat_axis=0, tiled=True)
    rows = arrived.reshape(pool_size * BLK, PIX_PAD)

    lifted = bf16_dot(rows, embed[0], NN) + bf16_dot(rows, embed[1], NN)
    scale = rms_scale(lifted)
    unit = lifted * scale
    normed_s = halves_of(unit * student_gain)
    pre = halved_dot(normed_s, up)
    cdf = 0.5 * (1.0 + lax.erf(pre * (2.0**-0.5)))
    act = halves_of(pre * cdf)
    slope = cdf + pre * jnp.exp(-0.5 * pre * pre) * ((2.0 * jnp.pi) ** -0.5)
    act, slope, *second = lax.optimization_barrier((act, slope, *second))
    back_across, ahead_across, low_near, high_near = second
    low = with_core([low_near, moved(back_across[:REST], x=1)])
    high = with_core([high_near, moved(ahead_across[REST:], x=-1)])
    near = with_core([shard, across, back, back_across, ahead, ahead_across])
    hidden = halves_of(lifted + halved_dot(act, down))
    student_out = halved_dot(hidden, head)

    embedded, context = teach(owners, rows, teacher_gain, gathered, near + low)
    core = lax.rem(lax.axis_index("student"), 2)
    core = core.reshape(1)
    *sums_a, down_rest, d_hidden, total = head_backward(
        core, owners, context, embedded, student_out, hidden, act, head, near + high
    )
    sent_a, d_hidden = lax.optimization_barrier((core_sum(*sums_a), d_hidden))
    chunk_a = chunk_sum(sent_a)
    sums_b = trunk_backward(
        core, d_hidden, slope, down, up, normed_s, unit, scale, student_gain[None], rows, down_rest, total
    )
    chunk_a, *sums_b = lax.optimization_barrier((chunk_a, *sums_b))
    chunk_b = keep_total(chunk_sum(core_sum(*sums_b)), core[0])
    chunks = jnp.concatenate([chunk_a.astype(jnp.bfloat16), chunk_b.astype(jnp.bfloat16)], axis=0)
    head_sum, down_sum, up_sum, embed_sum, gain_sum, cosine_sum = unpack_sums(
        core, *spread_chunk(chunks)
    )
    gain_sum = gain_sum[: D_S // LANES].reshape(D_S)
    mean_distance = 1.0 - jnp.sum(cosine_sum[7, :3]) / (DEVICES * 2 * BLK)
    return (mean_distance, embed_sum, gain_sum, up_sum, down_sum, head_sum)


def solution(mesh):
    in_specs = (
        P(("student", "pool"), None, None),
        P(("student", "pool"), None),
        P(("student", "pool"), None),
        P(),
        P(),
        P(),
        P(),
        P(),
        P("pool", None, "student"),
        P("pool", None),
        P("pool", None, "student"),
        P("pool", None, "student"),
    )
    out_specs = (P(), P(), P(), P(), P(), P())
    return jax.shard_map(
        on_device, mesh=mesh, in_specs=in_specs, out_specs=out_specs, check_vma=False
    )
```

```python
import jax
import jax.numpy as jnp
from jax import lax
from jax.experimental import pallas as pl
from jax.experimental.pallas import tpu as pltpu
from jax.sharding import PartitionSpec as P

HEADS = 24
HDIM = 64
EPSILON = 1e-06
BOTH = ("student", "pool")
DEVICES = 128
PAIR = 2 * HDIM
LANES = 128
PIX = 588
PIX_PAD = 640
D_S = 384
D_T = 1536
S_HID = 1536
BLK = 128
P_ROWS = 288
O_ROWS = 96
NEAR = 12
FAR = 4
CUT = 192
REST = P_ROWS - CUT
STUDENTS = 16
EMBED_PACK = 48
RANKS = DEVICES // 2
CHUNK = 64
SUM_ROWS = 2 * RANKS * CHUNK
EMBED_ROWS = 592
UP_AT = S_HID
EMBED_AT = UP_AT + D_S * S_HID // LANES
GAIN_AT = EMBED_AT + (D_S // LANES) * EMBED_ROWS
NT = (((1,), (1,)), ((), ()))
TN = (((0,), (0,)), ((), ()))
NN = (((1,), (0,)), ((), ()))


def bf16_dot(left, right, dims):
    return lax.dot_general(left, right, dims, preferred_element_type=jnp.float32)


def rms_scale(values):
    return lax.rsqrt(jnp.mean(values * values, axis=-1, keepdims=True) + EPSILON)


def halved_dot(left, right):
    return (
        bf16_dot(left[0], right[0], NN)
        + bf16_dot(left[1], right[0], NN)
        + bf16_dot(left[0], right[1], NN)
    )


def attend_block(mixed, at, out, base):
    lane = lax.broadcasted_iota(jnp.int32, (BLK, PAIR), 1)
    first = lane < HDIM
    zero = jnp.zeros((BLK, PAIR), jnp.bfloat16)
    ones = jnp.concatenate(
        [jnp.where(first, 1.0, 0.0), jnp.where(first, 0.0, 1.0)], axis=0
    ).astype(jnp.bfloat16)
    rows = pl.ds(at, BLK)
    for pair in range(HEADS // 2):
        start = pair * PAIR
        queries = mixed[rows, start : start + PAIR]
        keys = mixed[rows, D_T + start : D_T + start + PAIR]
        values = mixed[rows, 2 * D_T + start : 2 * D_T + start + PAIR]
        keys_two = jnp.concatenate(
            [jnp.where(first, keys, zero), jnp.where(first, zero, keys)], axis=0
        )
        values_two = jnp.concatenate(
            [jnp.where(first, values, zero), jnp.where(first, zero, values)], axis=0
        )
        scores = bf16_dot(queries, keys_two, NT)
        left, right = scores[:, :BLK], scores[:, BLK:]
        scale = HDIM ** (-0.5)
        left = jnp.exp((left - jnp.max(left, axis=1, keepdims=True)) * scale)
        right = jnp.exp((right - jnp.max(right, axis=1, keepdims=True)) * scale)
        weights = jnp.concatenate([left, right], axis=1).astype(jnp.bfloat16)
        summed = bf16_dot(weights, jnp.concatenate([values_two, ones], axis=1), NN)
        out[rows, start : start + PAIR] = (summed[:, :PAIR] / summed[:, PAIR:]).astype(jnp.bfloat16)


def shard_copies(plan, owners, target, semaphores, count):
    copies = []
    for i, (piece, start, rows, row) in enumerate(plan):
        at = pl.multiple_of(owners[i] * count + row, 16)
        copies.append(
            pltpu.make_async_copy(
                piece.at[pl.ds(start, rows)], target.at[pl.ds(at, rows)], semaphores.at[i]
            )
        )
    return copies


def teacher_kernel(owners, rows, gain, gathered, *rest):
    pieces, rest = rest[: NEAR + FAR], rest[NEAR + FAR :]
    embedded, context, embed, project, normed, mixed, semaphores, others = rest
    wide = D_T // 2
    first = [
        pltpu.make_async_copy(
            gathered.at[:, pl.ds(CUT, EMBED_PACK), pl.ds(i * wide, wide)], embed.at[:, i], others.at[i]
        )
        for i in range(2)
    ]
    for copy in first:
        copy.start()
    copies = [
        pltpu.make_async_copy(
            gathered.at[i, pl.ds(0, CUT)], project.at[pl.ds(i * P_ROWS, CUT)], others.at[2 + i]
        )
        for i in range(STUDENTS)
    ]
    plan = [(piece, 0, P_ROWS - CUT, CUT) for piece in pieces]
    copies += shard_copies(plan, owners, project, semaphores, P_ROWS)
    for copy in copies:
        copy.start()
    for copy in first:
        copy.wait()
    step = 2 * BLK

    @pl.loop(0, rows.shape[0] // step)
    def _(r):
        at = pl.ds(pl.multiple_of(r * step, step), step)
        weights = embed[...].reshape(D_T, wide)[:, :PIX_PAD]
        product = bf16_dot(rows[at, :], weights, NT)
        embedded[at, :] = product
        normed[at, :] = (product * scale_of(product) * gain[...]).astype(jnp.bfloat16)

    for copy in copies:
        copy.wait()
    tile = 512

    @pl.loop(0, 3 * D_T // tile)
    def _(n):
        at = pl.ds(pl.multiple_of(n * tile, tile), tile)
        mixed[:, at] = bf16_dot(normed[...], project[at, :], NT).astype(jnp.bfloat16)

    @pl.loop(0, rows.shape[0] // BLK)
    def _(b):
        at = pl.multiple_of(b * BLK, BLK)
        attend_block(mixed, at, context, at)


def teach(owners, rows, gain, gathered, pieces):
    count = rows.shape[0]
    vmem = pl.BlockSpec(memory_space=pltpu.VMEM)
    return pl.pallas_call(
        teacher_kernel,
        in_specs=[pl.BlockSpec(memory_space=pltpu.SMEM)] + [vmem] * 2
        + [pl.BlockSpec(memory_space=pl.ANY)] * (1 + NEAR + FAR),
        out_specs=[vmem] * 2,
        out_shape=[
            jax.ShapeDtypeStruct((count, D_T), jnp.float32),
            jax.ShapeDtypeStruct((count, D_T), jnp.bfloat16),
        ],
        scratch_shapes=[
            pltpu.VMEM((STUDENTS, 2, EMBED_PACK, D_T // 2), jnp.bfloat16),
            pltpu.VMEM((3 * D_T, D_T), jnp.bfloat16),
            pltpu.VMEM((count, D_T), jnp.bfloat16),
            pltpu.VMEM((count, 3 * D_T), jnp.bfloat16),
            pltpu.SemaphoreType.DMA((NEAR + FAR,)),
            pltpu.SemaphoreType.DMA((2 + STUDENTS,)),
        ],
        compiler_params=pltpu.CompilerParams(vmem_limit_bytes=58 * 1024 * 1024),
        cost_estimate=pl.CostEstimate(
            flops=2 * count * D_T * (PIX_PAD + 3 * D_T), bytes_accessed=30 * 1024 * 1024, transcendentals=0
        ),
        name="teacher",
    )(owners, rows, gain, gathered, *pieces)


def place(device):
    student, pool = device // 8, device % 8
    return [student // 4, student // 2 % 2, student % 2, pool]


def moved(values, x=0, z=0, core=0):
    pairs = []
    for device in range(DEVICES):
        at = place(device)
        student = ((at[0] + x) % 4 * 2 + (at[1] ^ z)) * 2 + (at[2] ^ core)
        pairs.append((device, student * 8 + at[3]))
    return lax.ppermute(values, BOTH, pairs)


def with_core(pieces):
    return pieces + [moved(values, core=1) for values in pieces]


def shard_owners():
    x, z, core, _ = place(lax.axis_index("student") * 8)

    def index(dx, dz, dc):
        return (lax.rem(x + dx + 4, 4) * 2 + (z + dz) % 2) * 2 + (core + dc) % 2

    near = [index(dx, dz, dc) for dc in range(2) for dx in (0, -1, 1) for dz in range(2)]
    far = [index(2, dz, dc) for dc in range(2) for dz in range(2)]
    return jnp.stack(near + far).astype(jnp.int32)


def core_groups():
    groups = [[], []]
    for device in range(DEVICES):
        groups[(device // 8) % 2].append(device)
    return groups


def core_swap(values):
    pairs = [(d, d ^ 8) for d in range(DEVICES)]
    return lax.ppermute(values, BOTH, pairs)


def halves_of(values):
    high = lax.reduce_precision(values, 8, 7)
    return high.astype(jnp.bfloat16), (values - high).astype(jnp.bfloat16)


def cut(values):
    high = values.astype(jnp.bfloat16)
    return high, (values - high.astype(jnp.float32)).astype(jnp.bfloat16)


def three_parts(value, lane):
    first = value.astype(jnp.bfloat16).astype(jnp.float32)
    second = (value - first).astype(jnp.bfloat16).astype(jnp.float32)
    third = value - first - second
    row = jnp.where(lane == 0, first, jnp.where(lane == 1, second, third))
    return jnp.where(lane < 3, row, 0.0)


def dot_three(left, right, dims):
    at_left, at_right = dims[0][0][0], dims[0][1][0]
    wide = jnp.concatenate([left[0], left[1], left[0]], axis=at_left)
    other = jnp.concatenate([right[0], right[0], right[1]], axis=at_right)
    return bf16_dot(wide, other, dims)


def scale_of(values):
    return lax.rsqrt(jnp.mean(values * values, axis=1, keepdims=True) + EPSILON)


def hand_over(core, sums, mine, other, done):
    half = SUM_ROWS // 2
    at = pl.multiple_of(core * half, half)
    across = pl.multiple_of((1 - core) * half, half)
    copies = [
        pltpu.make_async_copy(sums.at[pl.ds(across, half)], other, done.at[0]),
        pltpu.make_async_copy(sums.at[pl.ds(at, half)], mine, done.at[1]),
    ]
    for copy in copies:
        copy.start()
    for copy in copies:
        copy.wait()


def head_kernel(
    core, owners, context, embedded, student_out, hidden_hi, hidden_lo, act_hi, act_lo, head_hi, head_lo,
    *rest,
):
    pieces, rest = rest[: NEAR + FAR], rest[NEAR + FAR :]
    mine, other, down_rest, d_hidden_out, total, sums, output, semaphores, done = rest

    @pl.when(pl.program_id(0) == 0)
    def _():
        plan = [(piece, REST if i < NEAR else 0, O_ROWS, 0) for i, piece in enumerate(pieces)]
        copies = shard_copies(plan, owners, output, semaphores, O_ROWS)
        for copy in copies:
            copy.start()
        for copy in copies:
            copy.wait()
        sums[...] = jnp.zeros_like(sums)
        down_rest[...] = jnp.zeros_like(down_rest)
        total[...] = jnp.zeros_like(total)

    finished = embedded[...] + bf16_dot(context[...], output[...], NT)
    features = (finished * scale_of(finished)).astype(jnp.bfloat16).astype(jnp.float32)
    out = student_out[...]
    dot_mean = jnp.mean(out * features, axis=1, keepdims=True)
    out_scale, feature_scale = scale_of(out), scale_of(features)
    both = out_scale * feature_scale
    total[...] += jnp.sum(dot_mean * both)
    along = both * (-1.0 / D_T)
    back = both * dot_mean * out_scale * out_scale * (1.0 / D_T)
    d_out = cut(along * features + back * out)
    grad_head = dot_three((hidden_hi[...], hidden_lo[...]), d_out, TN)
    for i in range(D_T // LANES):
        sums[i * D_S : (i + 1) * D_S, :] += grad_head[:, i * LANES : (i + 1) * LANES]
    d_hidden = dot_three(d_out, (head_hi[...], head_lo[...]), NT)
    d_hidden_out[...] = d_hidden
    grad_down = dot_three((act_hi[...], act_lo[...]), cut(d_hidden), TN)
    at = D_S * D_T // LANES
    for i in range(2):
        sums[at + i * S_HID : at + (i + 1) * S_HID, :] += grad_down[:, i * LANES : (i + 1) * LANES]
    down_rest[...] += grad_down[:, 2 * LANES :]

    @pl.when(pl.program_id(0) == pl.num_programs(0) - 1)
    def _():
        hand_over(core[0], sums, mine, other, done)


def head_backward(core, owners, context, embedded, student_out, hidden, act, head, pieces):
    rows = context.shape[0]
    block = 256

    def by_row(columns):
        return pl.BlockSpec((block, columns), lambda r: (r, 0))

    def whole(shape):
        return pl.BlockSpec(shape, lambda r: (0, 0))

    return pl.pallas_call(
        head_kernel,
        grid=(rows // block,),
        in_specs=[
            pl.BlockSpec(memory_space=pltpu.SMEM),
            pl.BlockSpec(memory_space=pltpu.SMEM),
            by_row(D_T), by_row(D_T), by_row(D_T), by_row(D_S), by_row(D_S),
            by_row(S_HID), by_row(S_HID), whole((D_S, D_T)), whole((D_S, D_T)),
        ]
        + [pl.BlockSpec(memory_space=pl.ANY)] * (NEAR + FAR),
        out_specs=[pl.BlockSpec(memory_space=pl.ANY)] * 2
        + [whole((S_HID, LANES)), by_row(D_S), whole((8, LANES))],
        out_shape=[
            jax.ShapeDtypeStruct((SUM_ROWS // 2, LANES), jnp.float32),
            jax.ShapeDtypeStruct((SUM_ROWS // 2, LANES), jnp.float32),
            jax.ShapeDtypeStruct((S_HID, LANES), jnp.float32),
            jax.ShapeDtypeStruct((rows, D_S), jnp.float32),
            jax.ShapeDtypeStruct((8, LANES), jnp.float32),
        ],
        scratch_shapes=[
            pltpu.VMEM((SUM_ROWS, LANES), jnp.float32),
            pltpu.VMEM((D_T, D_T), jnp.bfloat16),
            pltpu.SemaphoreType.DMA((NEAR + FAR,)),
            pltpu.SemaphoreType.DMA((2,)),
        ],
        compiler_params=pltpu.CompilerParams(vmem_limit_bytes=56 * 1024 * 1024),
        cost_estimate=pl.CostEstimate(
            flops=2 * rows * D_T * (D_T + 9 * D_S), bytes_accessed=40 * 1024 * 1024, transcendentals=0
        ),
        name="head_backward",
    )(core, owners, context, embedded, student_out, *hidden, *act, *head, *pieces)


def trunk_kernel(
    core, d_hidden, slope, down_hi, down_lo, up_hi, up_lo, normed_hi, normed_lo, unit, scale, gain, rows,
    down_rest, total, mine, other, sums, dh_hi, dh_lo, d_normed, done,
):
    step = pl.program_id(0)
    tile = slope.shape[1]

    @pl.when(step == 0)
    def _():
        dh_hi[...], dh_lo[...] = cut(d_hidden[...])
        d_normed[...] = jnp.zeros_like(d_normed)
        sums[:UP_AT, :] = down_rest[...]
        sums[GAIN_AT:, :] = jnp.zeros((SUM_ROWS - GAIN_AT, LANES), jnp.float32)

    d_act = dot_three((dh_hi[...], dh_lo[...]), (down_hi[...], down_lo[...]), NT)
    d_pre = cut(d_act * slope[...])
    grad_up = dot_three((normed_hi[...], normed_lo[...]), d_pre, TN)
    at = pl.multiple_of(UP_AT + step * (tile // LANES) * D_S, LANES)
    for i in range(tile // LANES):
        sums[pl.ds(at + i * D_S, D_S), :] = grad_up[:, i * LANES : (i + 1) * LANES]
    d_normed[...] += dot_three(d_pre, (up_hi[...], up_lo[...]), NT)

    @pl.when(step == pl.num_programs(0) - 1)
    def _():
        d_out = d_normed[...]
        across = unit[...]
        grad_gain = jnp.sum(d_out * across, axis=0, keepdims=True)
        d_unit = d_out * gain[...]
        inner = jnp.mean(d_unit * across, axis=1, keepdims=True)
        d_lifted = cut(d_hidden[...] + scale[...] * (d_unit - across * inner))
        grad_embed = bf16_dot(rows[...], d_lifted[0], TN) + bf16_dot(rows[...], d_lifted[1], TN)
        for i in range(D_S // LANES):
            columns = slice(i * LANES, (i + 1) * LANES)
            start = EMBED_AT + i * EMBED_ROWS
            sums[start : start + EMBED_ROWS, :] = grad_embed[:EMBED_ROWS, columns]
            sums[GAIN_AT + i : GAIN_AT + i + 1, :] = grad_gain[:, columns]
        lane = lax.broadcasted_iota(jnp.int32, (1, LANES), 1)
        sums[SUM_ROWS - 1 :, :] = three_parts(total[0:1, :], lane)
        hand_over(core[0], sums, mine, other, done)


def trunk_backward(core, d_hidden, slope, down, up, normed, unit, scale, gain, rows, down_rest, total):
    count = d_hidden.shape[0]
    tile = 512

    def whole(values):
        return pl.BlockSpec(values.shape, lambda j: (0, 0))

    down_spec = pl.BlockSpec((tile, D_S), lambda j: (j, 0))
    up_spec = pl.BlockSpec((D_S, tile), lambda j: (0, j))
    return pl.pallas_call(
        trunk_kernel,
        grid=(S_HID // tile,),
        in_specs=[
            pl.BlockSpec(memory_space=pltpu.SMEM),
            whole(d_hidden), pl.BlockSpec((count, tile), lambda j: (0, j)),
            down_spec, down_spec, up_spec, up_spec,
            whole(normed[0]), whole(normed[1]), whole(unit), whole(scale), whole(gain), whole(rows),
            whole(down_rest), whole(total),
        ],
        out_specs=[pl.BlockSpec(memory_space=pl.ANY)] * 2,
        out_shape=[jax.ShapeDtypeStruct((SUM_ROWS // 2, LANES), jnp.float32)] * 2,
        scratch_shapes=[
            pltpu.VMEM((SUM_ROWS, LANES), jnp.float32),
            pltpu.VMEM((count, D_S), jnp.bfloat16),
            pltpu.VMEM((count, D_S), jnp.bfloat16),
            pltpu.VMEM((count, D_S), jnp.float32),
            pltpu.SemaphoreType.DMA((2,)),
        ],
        compiler_params=pltpu.CompilerParams(vmem_limit_bytes=56 * 1024 * 1024),
        cost_estimate=pl.CostEstimate(
            flops=2 * count * D_S * (9 * S_HID + 2 * PIX_PAD), bytes_accessed=30 * 1024 * 1024, transcendentals=0
        ),
        name="trunk_backward",
    )(core, d_hidden, slope, *down, *up, *normed, unit, scale, gain, rows, down_rest, total)


def unpack_kernel(core, mine, theirs, head, down, up, embed, gain, mean_distance):
    def unpack(low, high):
        def take(part, start, count):
            pieces, stop = [], start + count
            while start < stop:
                rank, row = start // CHUNK, start % CHUNK
                ref = low if rank < RANKS else high
                size = min(CHUNK - row, stop - start)
                at = part * CHUNK + row
                pieces.append(ref[rank % RANKS, at : at + size, :].astype(jnp.float32))
                start += size
            return pieces[0] if len(pieces) == 1 else jnp.concatenate(pieces, axis=0)

        for i in range(D_T // LANES):
            columns = slice(i * LANES, (i + 1) * LANES)
            head[:, columns] = take(0, i * D_S, D_S)
            up[:, columns] = take(1, UP_AT + i * D_S, D_S)
        at = D_S * D_T // LANES
        for i in range(2):
            down[:, i * LANES : (i + 1) * LANES] = take(0, at + i * S_HID, S_HID)
        down[:, 2 * LANES :] = take(1, 0, S_HID)
        for i in range(D_S // LANES):
            columns = slice(i * LANES, (i + 1) * LANES)
            embed[:, columns] = take(1, EMBED_AT + i * EMBED_ROWS, EMBED_ROWS)[:PIX]
        gains = take(1, GAIN_AT, 16)
        for i in range(D_S // LANES):
            gain[:, i * LANES : (i + 1) * LANES] = gains[i : i + 1]
        lane = lax.broadcasted_iota(jnp.int32, (1, LANES), 1)
        cosines = jnp.where(lane < 3, take(1, SUM_ROWS - 16, 16)[15:], 0.0)
        mean_distance[...] = 1.0 - jnp.sum(cosines, axis=1, keepdims=True) / (DEVICES * 2 * BLK)

    @pl.when(core[0] == 0)
    def _():
        unpack(mine, theirs)

    @pl.when(core[0] == 1)
    def _():
        unpack(theirs, mine)


def unpack_sums(core, mine, theirs):
    vmem = pl.BlockSpec(memory_space=pltpu.VMEM)
    shapes = [(D_S, D_T), (S_HID, D_S), (D_S, S_HID), (PIX, D_S), (1, D_S), (1, 1)]
    return pl.pallas_call(
        unpack_kernel,
        in_specs=[pl.BlockSpec(memory_space=pltpu.SMEM)] + [vmem] * 2,
        out_specs=[vmem] * 6,
        out_shape=[jax.ShapeDtypeStruct(shape, jnp.float32) for shape in shapes],
        compiler_params=pltpu.CompilerParams(vmem_limit_bytes=56 * 1024 * 1024),
        cost_estimate=pl.CostEstimate(flops=0, bytes_accessed=12 * 1024 * 1024, transcendentals=0),
        name="unpack_sums",
    )(core, mine, theirs)


def core_sum(mine, theirs):
    return (mine + theirs).astype(jnp.bfloat16).reshape(RANKS, CHUNK, LANES)


def to_all_ranks(values):
    return lax.all_to_all(values, BOTH, 0, 0, axis_index_groups=core_groups(), tiled=True)


def chunk_kernel(owner, got, spread):
    chunk = jnp.sum(got[...].astype(jnp.float32), axis=0)
    lane = lax.broadcasted_iota(jnp.int32, (1, LANES), 1)
    parts = chunk[2 * CHUNK - 1 :, :]
    whole = jnp.sum(jnp.where(lane < 3, parts, 0.0), axis=1, keepdims=True)
    last = jnp.where(owner[0] == 1, three_parts(whole, lane), parts)
    rounded = jnp.concatenate([chunk[: 2 * CHUNK - 1, :], last], axis=0).astype(jnp.bfloat16)
    spread[...] = jnp.broadcast_to(rounded[None], spread.shape)


def add_chunk(owner, got):
    vmem = pl.BlockSpec(memory_space=pltpu.VMEM)
    return pl.pallas_call(
        chunk_kernel,
        in_specs=[pl.BlockSpec(memory_space=pltpu.SMEM), vmem],
        out_specs=vmem,
        out_shape=jax.ShapeDtypeStruct(got.shape, jnp.bfloat16),
        compiler_params=pltpu.CompilerParams(vmem_limit_bytes=32 * 1024 * 1024),
        cost_estimate=pl.CostEstimate(flops=0, bytes_accessed=4 * 1024 * 1024, transcendentals=0),
        name="add_chunk",
    )(owner, got)


def on_device(
    pixels,
    keyframes,
    destination,
    student_embed,
    student_gain,
    student_up,
    student_down,
    student_head,
    teacher_embed,
    teacher_gain,
    teacher_project,
    teacher_output,
):
    pool_size = lax.axis_size("pool")

    project = teacher_project[0].T
    embed_shard = jnp.pad(teacher_embed[0].T, ((0, 0), (0, D_T // 2 - PIX)))
    embed_shard = jnp.concatenate([embed_shard[:EMBED_PACK], embed_shard[EMBED_PACK:]], axis=1)
    gathered = lax.all_gather(
        jnp.concatenate([project[:CUT], embed_shard], axis=0), "student", axis=0, tiled=False
    )
    shard = jnp.concatenate([project[CUT:], teacher_output[0].T], axis=0)
    first = [moved(shard, z=1), moved(shard, x=1), moved(shard, x=-1)]

    owners = shard_owners()

    teachers = jnp.arange(pool_size, dtype=jnp.int32)[:, None, None]
    chosen = [
        lax.dynamic_index_in_dim(pixels, keyframes[0, k], 0, keepdims=True) for k in range(2)
    ]
    outgoing = jnp.where(
        destination[0, 0] == teachers,
        chosen[0],
        jnp.where(destination[0, 1] == teachers, chosen[1], jnp.zeros((), jnp.bfloat16)),
    )
    outgoing = jnp.pad(outgoing, ((0, 0), (0, 0), (0, PIX_PAD - PIX)))
    up, down, head = halves_of(student_up), halves_of(student_down), halves_of(student_head)
    embed = halves_of(jnp.pad(student_embed, ((0, PIX_PAD - PIX), (0, 0))))
    outgoing, up, down, head, embed, *first = lax.optimization_barrier(
        (outgoing, up, down, head, embed, *first)
    )
    across, back, ahead = first
    second = [
        moved(across, x=1), moved(across, x=-1), moved(back[:REST], x=1), moved(ahead[REST:], x=-1)
    ]
    arrived = lax.all_to_all(outgoing, "pool", split_axis=0, concat_axis=0, tiled=True)
    rows = arrived.reshape(pool_size * BLK, PIX_PAD)

    lifted = bf16_dot(rows, embed[0], NN) + bf16_dot(rows, embed[1], NN)
    scale = rms_scale(lifted)
    unit = lifted * scale
    normed_s = halves_of(unit * student_gain)
    pre = halved_dot(normed_s, up)
    cdf = 0.5 * (1.0 + lax.erf(pre * (2.0**-0.5)))
    act = halves_of(pre * cdf)
    slope = cdf + pre * jnp.exp(-0.5 * pre * pre) * ((2.0 * jnp.pi) ** -0.5)
    act, slope, *second = lax.optimization_barrier((act, slope, *second))
    back_across, ahead_across, low_near, high_near = second
    low = with_core([low_near, moved(back_across[:REST], x=1)])
    high = with_core([high_near, moved(ahead_across[REST:], x=-1)])
    near = with_core([shard, across, back, back_across, ahead, ahead_across])
    hidden = halves_of(lifted + halved_dot(act, down))
    student_out = halved_dot(hidden, head)

    embedded, context = teach(owners, rows, teacher_gain, gathered, near + low)
    core = lax.rem(lax.axis_index("student"), 2)
    core = core.reshape(1)
    *sums_a, down_rest, d_hidden, total = head_backward(
        core, owners, context, embedded, student_out, hidden, act, head, near + high
    )
    theirs_a = core_swap(sums_a[1])
    sums_b = trunk_backward(
        core, d_hidden, slope, down, up, normed_s, unit, scale, student_gain[None], rows, down_rest, total
    )
    rank = lax.axis_index("student") // 2 * 8 + lax.axis_index("pool")
    owner = jnp.logical_and(core == 1, rank == RANKS - 1).astype(jnp.int32)
    theirs_a, *sums_b = lax.optimization_barrier((theirs_a, *sums_b))
    sent = [core_sum(sums_a[0], theirs_a), core_sum(sums_b[0], core_swap(sums_b[1]))]
    got = to_all_ranks(jnp.concatenate(sent, axis=1))
    half = to_all_ranks(add_chunk(owner, got))
    head_sum, down_sum, up_sum, embed_sum, gain_sum, mean_distance = unpack_sums(
        core, half, core_swap(half)
    )
    return (mean_distance.reshape(()), embed_sum, gain_sum.reshape(D_S), up_sum, down_sum, head_sum)


def solution(mesh):
    in_specs = (
        P(("student", "pool"), None, None),
        P(("student", "pool"), None),
        P(("student", "pool"), None),
        P(),
        P(),
        P(),
        P(),
        P(),
        P("pool", None, "student"),
        P("pool", None),
        P("pool", None, "student"),
        P("pool", None, "student"),
    )
    out_specs = (P(), P(), P(), P(), P(), P())
    return jax.shard_map(
        on_device, mesh=mesh, in_specs=in_specs, out_specs=out_specs, check_vma=False
    )
```

```python
import jax
import jax.numpy as jnp
from jax import lax
from jax.experimental import pallas as pl
from jax.experimental.pallas import tpu as pltpu
from jax.sharding import PartitionSpec as P

HEADS = 24
HDIM = 64
EPSILON = 1e-06
BOTH = ("student", "pool")
DEVICES = 128
PAIR = 2 * HDIM
LANES = 128
PIX = 588
PIX_PAD = 640
D_S = 384
D_T = 1536
S_HID = 1536
BLK = 128
P_ROWS = 288
O_ROWS = 96
NEAR = 12
FAR = 4
CUT = 192
REST = P_ROWS - CUT
STUDENTS = 16
EMBED_PACK = 48
RANKS = DEVICES // 2
CHUNK = 64
SUM_ROWS = 2 * RANKS * CHUNK
EMBED_ROWS = 592
UP_AT = S_HID
EMBED_AT = UP_AT + D_S * S_HID // LANES
GAIN_AT = EMBED_AT + (D_S // LANES) * EMBED_ROWS
NT = (((1,), (1,)), ((), ()))
TN = (((0,), (0,)), ((), ()))
NN = (((1,), (0,)), ((), ()))


def bf16_dot(left, right, dims):
    return lax.dot_general(left, right, dims, preferred_element_type=jnp.float32)


def rms_scale(values):
    return lax.rsqrt(jnp.mean(values * values, axis=-1, keepdims=True) + EPSILON)


def halved_dot(left, right):
    return (
        bf16_dot(left[0], right[0], NN)
        + bf16_dot(left[1], right[0], NN)
        + bf16_dot(left[0], right[1], NN)
    )


def attend_block(mixed, at, out):
    lane = lax.broadcasted_iota(jnp.int32, (BLK, PAIR), 1)
    first = lane < HDIM
    zero = jnp.zeros((BLK, PAIR), jnp.bfloat16)
    ones = jnp.concatenate(
        [jnp.where(first, 1.0, 0.0), jnp.where(first, 0.0, 1.0)], axis=0
    ).astype(jnp.bfloat16)
    rows = pl.ds(at, BLK)
    for pair in range(HEADS // 2):
        start = pair * PAIR
        queries = mixed[rows, start : start + PAIR]
        keys = mixed[rows, D_T + start : D_T + start + PAIR]
        values = mixed[rows, 2 * D_T + start : 2 * D_T + start + PAIR]
        keys_two = jnp.concatenate(
            [jnp.where(first, keys, zero), jnp.where(first, zero, keys)], axis=0
        )
        values_two = jnp.concatenate(
            [jnp.where(first, values, zero), jnp.where(first, zero, values)], axis=0
        )
        scores = bf16_dot(queries, keys_two, NT)
        left, right = scores[:, :BLK], scores[:, BLK:]
        scale = HDIM ** (-0.5)
        left = jnp.exp((left - jnp.max(left, axis=1, keepdims=True)) * scale)
        right = jnp.exp((right - jnp.max(right, axis=1, keepdims=True)) * scale)
        weights = jnp.concatenate([left, right], axis=1).astype(jnp.bfloat16)
        summed = bf16_dot(weights, jnp.concatenate([values_two, ones], axis=1), NN)
        out[rows, start : start + PAIR] = (summed[:, :PAIR] / summed[:, PAIR:]).astype(jnp.bfloat16)


def shard_copies(plan, owners, target, semaphores, count):
    copies = []
    for i, (piece, start, rows, row) in enumerate(plan):
        at = pl.multiple_of(owners[i] * count + row, 16)
        copies.append(
            pltpu.make_async_copy(
                piece.at[pl.ds(start, rows)], target.at[pl.ds(at, rows)], semaphores.at[i]
            )
        )
    return copies


def place(device):
    student, pool = device // 8, device % 8
    return [student // 4, student // 2 % 2, student % 2, pool]


def moved(values, x=0, z=0, core=0):
    pairs = []
    for device in range(DEVICES):
        at = place(device)
        student = ((at[0] + x) % 4 * 2 + (at[1] ^ z)) * 2 + (at[2] ^ core)
        pairs.append((device, student * 8 + at[3]))
    return lax.ppermute(values, BOTH, pairs)


def with_core(pieces):
    return pieces + [moved(values, core=1) for values in pieces]


def shard_owners():
    x, z, core, _ = place(lax.axis_index("student") * 8)

    def index(dx, dz, dc):
        return (lax.rem(x + dx + 4, 4) * 2 + (z + dz) % 2) * 2 + (core + dc) % 2

    near = [index(dx, dz, dc) for dc in range(2) for dx in (0, -1, 1) for dz in range(2)]
    far = [index(2, dz, dc) for dc in range(2) for dz in range(2)]
    return jnp.stack(near + far).astype(jnp.int32)


def core_groups():
    groups = [[], []]
    for device in range(DEVICES):
        groups[(device // 8) % 2].append(device)
    return groups


def core_swap(values):
    pairs = [(d, d ^ 8) for d in range(DEVICES)]
    return lax.ppermute(values, BOTH, pairs)


def halves_of(values):
    high = lax.reduce_precision(values, 8, 7)
    return high.astype(jnp.bfloat16), (values - high).astype(jnp.bfloat16)


def cut(values):
    high = values.astype(jnp.bfloat16)
    return high, (values - high.astype(jnp.float32)).astype(jnp.bfloat16)


def three_parts(value, lane):
    first = value.astype(jnp.bfloat16).astype(jnp.float32)
    second = (value - first).astype(jnp.bfloat16).astype(jnp.float32)
    third = value - first - second
    row = jnp.where(lane == 0, first, jnp.where(lane == 1, second, third))
    return jnp.where(lane < 3, row, 0.0)


def dot_three(left, right, dims):
    at_left, at_right = dims[0][0][0], dims[0][1][0]
    wide = jnp.concatenate([left[0], left[1], left[0]], axis=at_left)
    other = jnp.concatenate([right[0], right[0], right[1]], axis=at_right)
    return bf16_dot(wide, other, dims)


def scale_of(values):
    return lax.rsqrt(jnp.mean(values * values, axis=1, keepdims=True) + EPSILON)


def hand_over(core, sums, mine, other, done):
    half = SUM_ROWS // 2
    at = pl.multiple_of(core * half, half)
    across = pl.multiple_of((1 - core) * half, half)
    copies = [
        pltpu.make_async_copy(sums.at[pl.ds(across, half)], other, done.at[0]),
        pltpu.make_async_copy(sums.at[pl.ds(at, half)], mine, done.at[1]),
    ]
    for copy in copies:
        copy.start()
    for copy in copies:
        copy.wait()


def project_rows(refs, owners, scopes):
    rows, gain, gathered, pieces, embedded, mixed, semaphores, others = refs
    embed, project, normed = scopes
    wide = D_T // 2
    first = [
        pltpu.make_async_copy(
            gathered.at[:, pl.ds(CUT, EMBED_PACK), pl.ds(i * wide, wide)], embed.at[:, i], others.at[i]
        )
        for i in range(2)
    ]
    for copy in first:
        copy.start()
    copies = [
        pltpu.make_async_copy(
            gathered.at[i, pl.ds(0, CUT)], project.at[pl.ds(i * P_ROWS, CUT)], others.at[2 + i]
        )
        for i in range(STUDENTS)
    ]
    plan = [(piece, 0, REST, CUT) for piece in pieces]
    copies += shard_copies(plan, owners, project, semaphores, P_ROWS)
    for copy in copies:
        copy.start()
    for copy in first:
        copy.wait()
    step = 2 * BLK

    @pl.loop(0, rows.shape[0] // step)
    def _(r):
        at = pl.ds(pl.multiple_of(r * step, step), step)
        weights = embed[...].reshape(D_T, wide)[:, :PIX_PAD]
        product = bf16_dot(rows[at, :], weights, NT)
        embedded[at, :] = product
        normed[at, :] = (product * scale_of(product) * gain[...]).astype(jnp.bfloat16)

    for copy in copies:
        copy.wait()
    tile = 512

    @pl.loop(0, 3 * D_T // tile)
    def _(n):
        at = pl.ds(pl.multiple_of(n * tile, tile), tile)
        mixed[:, at] = bf16_dot(normed[...], project[at, :], NT).astype(jnp.bfloat16)


def teacher_kernel(core, project_owners, output_owners, rows, gain, gathered, *rest):
    pieces, rest = rest[: NEAR + FAR], rest[NEAR + FAR :]
    high, rest = rest[:FAR], rest[FAR:]
    sources, rest = rest[:7], rest[7:]
    mine, other, down_rest, d_hidden_out, total, embedded, context, mixed, *semaphores = rest
    project_done, others, output_done, sources_done, done = semaphores
    count, block = rows.shape[0], 2 * BLK

    def project(*scopes):
        refs = rows, gain, gathered, pieces, embedded, mixed, project_done, others
        project_rows(refs, project_owners, scopes)

    pl.run_scoped(
        project,
        pltpu.VMEM((STUDENTS, 2, EMBED_PACK, D_T // 2), jnp.bfloat16),
        pltpu.VMEM((3 * D_T, D_T), jnp.bfloat16),
        pltpu.VMEM((count, D_T), jnp.bfloat16),
    )

    def compare(output, sums, *held):
        plan = [(piece, REST if i < NEAR else 0, O_ROWS, 0) for i, piece in enumerate(pieces[:NEAR] + high)]
        copies = shard_copies(plan, output_owners, output, output_done, O_ROWS)
        copies += [
            pltpu.make_async_copy(source, target, sources_done.at[i])
            for i, (source, target) in enumerate(zip(sources, held))
        ]
        for copy in copies:
            copy.start()
        sums[...] = jnp.zeros_like(sums)
        down_rest[...] = jnp.zeros_like(down_rest)
        total[...] = jnp.zeros_like(total)

        @pl.loop(0, count // BLK)
        def _(b):
            attend_block(mixed, pl.multiple_of(b * BLK, BLK), context)

        for copy in copies:
            copy.wait()
        student_out, hidden_hi, hidden_lo, act_hi, act_lo, head_hi, head_lo = held

        @pl.loop(0, count // block)
        def _(r):
            at = pl.ds(pl.multiple_of(r * block, block), block)
            finished = embedded[at, :] + bf16_dot(context[at, :], output[...], NT)
            features = (finished * scale_of(finished)).astype(jnp.bfloat16).astype(jnp.float32)
            out = student_out[at, :]
            dot_mean = jnp.mean(out * features, axis=1, keepdims=True)
            out_scale, feature_scale = scale_of(out), scale_of(features)
            both = out_scale * feature_scale
            total[...] += jnp.sum(dot_mean * both)
            along = both * (-1.0 / D_T)
            back = both * dot_mean * out_scale * out_scale * (1.0 / D_T)
            d_out = cut(along * features + back * out)
            grad_head = dot_three((hidden_hi[at, :], hidden_lo[at, :]), d_out, TN)
            for i in range(D_T // LANES):
                sums[i * D_S : (i + 1) * D_S, :] += grad_head[:, i * LANES : (i + 1) * LANES]
            d_hidden = dot_three(d_out, (head_hi[...], head_lo[...]), NT)
            d_hidden_out[at, :] = d_hidden
            grad_down = dot_three((act_hi[at, :], act_lo[at, :]), cut(d_hidden), TN)
            start = D_S * D_T // LANES
            for i in range(2):
                columns = slice(i * LANES, (i + 1) * LANES)
                sums[start + i * S_HID : start + (i + 1) * S_HID, :] += grad_down[:, columns]
            down_rest[...] += grad_down[:, 2 * LANES :]

        hand_over(core[0], sums, mine, other, done)

    pl.run_scoped(
        compare,
        pltpu.VMEM((D_T, D_T), jnp.bfloat16),
        pltpu.VMEM((SUM_ROWS, LANES), jnp.float32),
        *[pltpu.VMEM(source.shape, source.dtype) for source in sources],
    )


def teacher_and_head(core, owners, rows, gain, gathered, pieces, high, student_out, hidden, act, head):
    count = rows.shape[0]
    smem, vmem, anywhere = [
        pl.BlockSpec(memory_space=space) for space in (pltpu.SMEM, pltpu.VMEM, pl.ANY)
    ]
    sources = (student_out, *hidden, *act, *head)
    return pl.pallas_call(
        teacher_kernel,
        in_specs=[smem] * 3 + [vmem] * 2 + [anywhere] * (1 + len(pieces) + len(high) + len(sources)),
        out_specs=[anywhere] * 2 + [vmem] * 3,
        out_shape=[
            jax.ShapeDtypeStruct((SUM_ROWS // 2, LANES), jnp.float32),
            jax.ShapeDtypeStruct((SUM_ROWS // 2, LANES), jnp.float32),
            jax.ShapeDtypeStruct((S_HID, LANES), jnp.float32),
            jax.ShapeDtypeStruct((count, D_S), jnp.float32),
            jax.ShapeDtypeStruct((8, LANES), jnp.float32),
        ],
        scratch_shapes=[
            pltpu.VMEM((count, D_T), jnp.float32),
            pltpu.VMEM((count, D_T), jnp.bfloat16),
            pltpu.VMEM((count, 3 * D_T), jnp.bfloat16),
            pltpu.SemaphoreType.DMA((NEAR + FAR,)),
            pltpu.SemaphoreType.DMA((2 + STUDENTS,)),
            pltpu.SemaphoreType.DMA((NEAR + FAR,)),
            pltpu.SemaphoreType.DMA((len(sources),)),
            pltpu.SemaphoreType.DMA((2,)),
        ],
        compiler_params=pltpu.CompilerParams(vmem_limit_bytes=60 * 1024 * 1024),
        cost_estimate=pl.CostEstimate(
            flops=2 * count * D_T * (PIX_PAD + 4 * D_T + 9 * D_S),
            bytes_accessed=50 * 1024 * 1024,
            transcendentals=0,
        ),
        name="teacher_and_head",
    )(core, owners, owners, rows, gain, gathered, *pieces, *high, *sources)


def trunk_kernel(
    core, d_hidden, slope, down_hi, down_lo, up_hi, up_lo, normed_hi, normed_lo, lifted, gain, rows,
    down_rest, total, mine, other, sums, dh_hi, dh_lo, d_normed, done,
):
    step = pl.program_id(0)
    tile = slope.shape[1]

    @pl.when(step == 0)
    def _():
        dh_hi[...], dh_lo[...] = cut(d_hidden[...])
        d_normed[...] = jnp.zeros_like(d_normed)
        sums[:UP_AT, :] = down_rest[...]
        sums[GAIN_AT:, :] = jnp.zeros((SUM_ROWS - GAIN_AT, LANES), jnp.float32)

    d_act = dot_three((dh_hi[...], dh_lo[...]), (down_hi[...], down_lo[...]), NT)
    d_pre = cut(d_act * slope[...])
    grad_up = dot_three((normed_hi[...], normed_lo[...]), d_pre, TN)
    at = pl.multiple_of(UP_AT + step * (tile // LANES) * D_S, LANES)
    for i in range(tile // LANES):
        sums[pl.ds(at + i * D_S, D_S), :] = grad_up[:, i * LANES : (i + 1) * LANES]
    d_normed[...] += dot_three(d_pre, (up_hi[...], up_lo[...]), NT)

    @pl.when(step == pl.num_programs(0) - 1)
    def _():
        d_out = d_normed[...]
        scale = scale_of(lifted[...])
        across = lifted[...] * scale
        grad_gain = jnp.sum(d_out * across, axis=0, keepdims=True)
        d_unit = d_out * gain[...]
        inner = jnp.mean(d_unit * across, axis=1, keepdims=True)
        d_lifted = cut(d_hidden[...] + scale * (d_unit - across * inner))
        grad_embed = bf16_dot(rows[...], d_lifted[0], TN) + bf16_dot(rows[...], d_lifted[1], TN)
        for i in range(D_S // LANES):
            columns = slice(i * LANES, (i + 1) * LANES)
            start = EMBED_AT + i * EMBED_ROWS
            sums[start : start + EMBED_ROWS, :] = grad_embed[:EMBED_ROWS, columns]
            sums[GAIN_AT + i : GAIN_AT + i + 1, :] = grad_gain[:, columns]
        lane = lax.broadcasted_iota(jnp.int32, (1, LANES), 1)
        sums[SUM_ROWS - 1 :, :] = three_parts(total[0:1, :], lane)
        hand_over(core[0], sums, mine, other, done)


def trunk_backward(core, d_hidden, slope, down, up, normed, lifted, gain, rows, down_rest, total):
    count = d_hidden.shape[0]
    tile = 512

    def whole(values):
        return pl.BlockSpec(values.shape, lambda j: (0, 0))

    down_spec = pl.BlockSpec((tile, D_S), lambda j: (j, 0))
    up_spec = pl.BlockSpec((D_S, tile), lambda j: (0, j))
    return pl.pallas_call(
        trunk_kernel,
        grid=(S_HID // tile,),
        in_specs=[
            pl.BlockSpec(memory_space=pltpu.SMEM),
            whole(d_hidden), pl.BlockSpec((count, tile), lambda j: (0, j)),
            down_spec, down_spec, up_spec, up_spec,
            whole(normed[0]), whole(normed[1]), whole(lifted), whole(gain), whole(rows),
            whole(down_rest), whole(total),
        ],
        out_specs=[pl.BlockSpec(memory_space=pl.ANY)] * 2,
        out_shape=[jax.ShapeDtypeStruct((SUM_ROWS // 2, LANES), jnp.float32)] * 2,
        scratch_shapes=[
            pltpu.VMEM((SUM_ROWS, LANES), jnp.float32),
            pltpu.VMEM((count, D_S), jnp.bfloat16),
            pltpu.VMEM((count, D_S), jnp.bfloat16),
            pltpu.VMEM((count, D_S), jnp.float32),
            pltpu.SemaphoreType.DMA((2,)),
        ],
        compiler_params=pltpu.CompilerParams(vmem_limit_bytes=56 * 1024 * 1024),
        cost_estimate=pl.CostEstimate(
            flops=2 * count * D_S * (9 * S_HID + 2 * PIX_PAD), bytes_accessed=30 * 1024 * 1024, transcendentals=0
        ),
        name="trunk_backward",
    )(core, d_hidden, slope, *down, *up, *normed, lifted, gain, rows, down_rest, total)


def unpack_kernel(
    core, mine_hbm, theirs_hbm, head_hbm, down_hbm, up_hbm, embed_hbm, gain, mean_distance,
    mine, theirs, head, down, up, embed, semaphores,
):
    arrivals = [
        pltpu.make_async_copy(mine_hbm, mine, semaphores.at[0]),
        pltpu.make_async_copy(theirs_hbm, theirs, semaphores.at[1]),
    ]
    results = [
        pltpu.make_async_copy(source, target, semaphores.at[2 + i])
        for i, (source, target) in enumerate(
            [(head, head_hbm), (down, down_hbm), (up, up_hbm), (embed, embed_hbm)]
        )
    ]
    for copy in arrivals:
        copy.start()
    for copy in arrivals:
        copy.wait()

    def take(halves, part, start, count):
        pieces, stop = [], start + count
        while start < stop:
            rank, row = start // CHUNK, start % CHUNK
            size = min(CHUNK - row, stop - start)
            at = part * CHUNK + row
            pieces.append(halves[rank // RANKS][rank % RANKS, at : at + size, :].astype(jnp.float32))
            start += size
        return pieces[0] if len(pieces) == 1 else jnp.concatenate(pieces, axis=0)

    def strip(i):
        return slice(i * LANES, (i + 1) * LANES)

    def unpack_head(halves):
        for i in range(D_T // LANES):
            head[:, strip(i)] = take(halves, 0, i * D_S, D_S)

    def unpack_down(halves):
        at = D_S * D_T // LANES
        for i in range(2):
            down[:, strip(i)] = take(halves, 0, at + i * S_HID, S_HID)
        down[:, 2 * LANES :] = take(halves, 1, 0, S_HID)

    def unpack_up(halves):
        for i in range(S_HID // LANES):
            up[:, strip(i)] = take(halves, 1, UP_AT + i * D_S, D_S)

    def unpack_rest(halves):
        for i in range(D_S // LANES):
            embed[:, strip(i)] = take(halves, 1, EMBED_AT + i * EMBED_ROWS, EMBED_ROWS)[:PIX]
        gains = take(halves, 1, GAIN_AT, 16)
        for i in range(D_S // LANES):
            gain[:, strip(i)] = gains[i : i + 1]
        lane = lax.broadcasted_iota(jnp.int32, (1, LANES), 1)
        cosines = jnp.where(lane < 3, take(halves, 1, SUM_ROWS - 16, 16)[15:], 0.0)
        mean_distance[0] = 1.0 - jnp.sum(cosines) * (1.0 / (DEVICES * 2 * BLK))

    for unpack, copy in zip([unpack_head, unpack_down, unpack_up, unpack_rest], results):

        @pl.when(core[0] == 0)
        def _():
            unpack((mine, theirs))

        @pl.when(core[0] == 1)
        def _():
            unpack((theirs, mine))

        copy.start()
    for copy in results:
        copy.wait()


def unpack_sums(core, mine, theirs):
    smem, vmem, anywhere = [
        pl.BlockSpec(memory_space=space) for space in (pltpu.SMEM, pltpu.VMEM, pl.ANY)
    ]
    shapes = [(D_S, D_T), (S_HID, D_S), (D_S, S_HID), (PIX, D_S)]
    return pl.pallas_call(
        unpack_kernel,
        in_specs=[smem, anywhere, anywhere],
        out_specs=[anywhere] * 4 + [vmem, smem],
        out_shape=[jax.ShapeDtypeStruct(shape, jnp.float32) for shape in shapes + [(1, D_S), (1,)]],
        scratch_shapes=[pltpu.VMEM(mine.shape, mine.dtype)] * 2
        + [pltpu.VMEM(shape, jnp.float32) for shape in shapes]
        + [pltpu.SemaphoreType.DMA((6,))],
        compiler_params=pltpu.CompilerParams(vmem_limit_bytes=56 * 1024 * 1024),
        cost_estimate=pl.CostEstimate(flops=0, bytes_accessed=12 * 1024 * 1024, transcendentals=0),
        name="unpack_sums",
    )(core, mine, theirs)


def core_sum(mine, theirs):
    return (mine + theirs).astype(jnp.bfloat16).reshape(RANKS, CHUNK, LANES)


def to_all_ranks(values):
    return lax.all_to_all(values, BOTH, 0, 0, axis_index_groups=core_groups(), tiled=True)


def chunk_kernel(owner, got, spread):
    chunk = jnp.sum(got[...].astype(jnp.float32), axis=0)
    lane = lax.broadcasted_iota(jnp.int32, (1, LANES), 1)
    parts = chunk[2 * CHUNK - 1 :, :]
    whole = jnp.sum(jnp.where(lane < 3, parts, 0.0), axis=1, keepdims=True)
    last = jnp.where(owner[0] == 1, three_parts(whole, lane), parts)
    rounded = jnp.concatenate([chunk[: 2 * CHUNK - 1, :], last], axis=0).astype(jnp.bfloat16)
    spread[...] = jnp.broadcast_to(rounded[None], spread.shape)


def add_chunk(owner, got):
    vmem = pl.BlockSpec(memory_space=pltpu.VMEM)
    return pl.pallas_call(
        chunk_kernel,
        in_specs=[pl.BlockSpec(memory_space=pltpu.SMEM), vmem],
        out_specs=vmem,
        out_shape=jax.ShapeDtypeStruct(got.shape, jnp.bfloat16),
        compiler_params=pltpu.CompilerParams(vmem_limit_bytes=32 * 1024 * 1024),
        cost_estimate=pl.CostEstimate(flops=0, bytes_accessed=4 * 1024 * 1024, transcendentals=0),
        name="add_chunk",
    )(owner, got)


def on_device(
    pixels,
    keyframes,
    destination,
    student_embed,
    student_gain,
    student_up,
    student_down,
    student_head,
    teacher_embed,
    teacher_gain,
    teacher_project,
    teacher_output,
):
    pool_size = lax.axis_size("pool")

    project = teacher_project[0].T
    embed_shard = jnp.pad(teacher_embed[0].T, ((0, 0), (0, D_T // 2 - PIX)))
    embed_shard = jnp.concatenate([embed_shard[:EMBED_PACK], embed_shard[EMBED_PACK:]], axis=1)
    gathered = lax.all_gather(
        jnp.concatenate([project[:CUT], embed_shard], axis=0), "student", axis=0, tiled=False
    )
    shard = jnp.concatenate([project[CUT:], teacher_output[0].T], axis=0)
    first = [moved(shard, z=1), moved(shard, x=1), moved(shard, x=-1)]

    owners = shard_owners()

    teachers = jnp.arange(pool_size, dtype=jnp.int32)[:, None, None]
    chosen = [
        lax.dynamic_index_in_dim(pixels, keyframes[0, k], 0, keepdims=True) for k in range(2)
    ]
    outgoing = jnp.where(
        destination[0, 0] == teachers,
        chosen[0],
        jnp.where(destination[0, 1] == teachers, chosen[1], jnp.zeros((), jnp.bfloat16)),
    )
    outgoing = jnp.pad(outgoing, ((0, 0), (0, 0), (0, PIX_PAD - PIX)))
    up, down, head = halves_of(student_up), halves_of(student_down), halves_of(student_head)
    embed = halves_of(jnp.pad(student_embed, ((0, PIX_PAD - PIX), (0, 0))))
    outgoing, up, down, head, embed, gain, *first = lax.optimization_barrier(
        (outgoing, up, down, head, embed, student_gain[None], *first)
    )
    across, back, ahead = first
    second = [
        moved(across, x=1), moved(across, x=-1), moved(back[:REST], x=1), moved(ahead[REST:], x=-1)
    ]
    arrived = lax.all_to_all(outgoing, "pool", split_axis=0, concat_axis=0, tiled=True)
    rows = arrived.reshape(pool_size * BLK, PIX_PAD)

    lifted = bf16_dot(rows, embed[0], NN) + bf16_dot(rows, embed[1], NN)
    normed_s = halves_of(lifted * rms_scale(lifted) * student_gain)
    pre = halved_dot(normed_s, up)
    cdf = 0.5 * (1.0 + lax.erf(pre * (2.0**-0.5)))
    act = halves_of(pre * cdf)
    slope = cdf + pre * jnp.exp(-0.5 * pre * pre) * ((2.0 * jnp.pi) ** -0.5)
    act, slope, *second = lax.optimization_barrier((act, slope, *second))
    back_across, ahead_across, low_near, high_near = second
    third = [moved(back_across[:REST], x=1), moved(ahead_across[REST:], x=-1)]
    near = with_core([shard, across, back, back_across, ahead, ahead_across])
    hidden = halves_of(lifted + halved_dot(act, down))
    student_out = halved_dot(hidden, head)
    student_out, *third = lax.optimization_barrier((student_out, *third))
    low = with_core([low_near, third[0]])
    high = with_core([high_near, third[1]])

    core = lax.rem(lax.axis_index("student"), 2).reshape(1)
    *sums_a, down_rest, d_hidden, total = teacher_and_head(
        core, owners, rows, teacher_gain, gathered, near + low, high, student_out, hidden, act, head
    )
    theirs_a = core_swap(sums_a[1])
    sums_b = trunk_backward(
        core, d_hidden, slope, down, up, normed_s, lifted, gain, rows, down_rest, total
    )
    rank = lax.axis_index("student") // 2 * 8 + lax.axis_index("pool")
    owner = jnp.logical_and(core == 1, rank == RANKS - 1).astype(jnp.int32)
    theirs_a, *sums_b = lax.optimization_barrier((theirs_a, *sums_b))
    sent = [core_sum(sums_a[0], theirs_a), core_sum(sums_b[0], core_swap(sums_b[1]))]
    got = to_all_ranks(jnp.concatenate(sent, axis=1))
    half = to_all_ranks(add_chunk(owner, got))
    head_sum, down_sum, up_sum, embed_sum, gain_sum, mean_distance = unpack_sums(
        core, half, core_swap(half)
    )
    return (mean_distance.reshape(()), embed_sum, gain_sum.reshape(D_S), up_sum, down_sum, head_sum)


def solution(mesh):
    in_specs = (
        P(("student", "pool"), None, None),
        P(("student", "pool"), None),
        P(("student", "pool"), None),
        P(),
        P(),
        P(),
        P(),
        P(),
        P("pool", None, "student"),
        P("pool", None),
        P("pool", None, "student"),
        P("pool", None, "student"),
    )
    out_specs = (P(), P(), P(), P(), P(), P())
    return jax.shard_map(
        on_device, mesh=mesh, in_specs=in_specs, out_specs=out_specs, check_vma=False
    )
```

```python
import jax
import jax.numpy as jnp
from jax import lax
from jax.experimental import pallas as pl
from jax.experimental.pallas import tpu as pltpu
from jax.sharding import PartitionSpec as P

HEADS = 24
HDIM = 64
EPSILON = 1e-06
BOTH = ("student", "pool")
DEVICES = 128
PAIR = 2 * HDIM
LANES = 128
PIX = 588
PIX_PAD = 640
D_S = 384
D_T = 1536
S_HID = 1536
BLK = 128
P_ROWS = 288
O_ROWS = 96
NEAR = 12
FAR = 4
CUT = 192
REST = P_ROWS - CUT
STUDENTS = 16
EMBED_PACK = 48
RANKS = DEVICES // 2
CHUNK = 64
SUM_ROWS = 2 * RANKS * CHUNK
EMBED_ROWS = 592
UP_AT = S_HID
EMBED_AT = UP_AT + D_S * S_HID // LANES
GAIN_AT = EMBED_AT + (D_S // LANES) * EMBED_ROWS
NT = (((1,), (1,)), ((), ()))
TN = (((0,), (0,)), ((), ()))
NN = (((1,), (0,)), ((), ()))


def bf16_dot(left, right, dims):
    return lax.dot_general(left, right, dims, preferred_element_type=jnp.float32)


def rms_scale(values):
    return lax.rsqrt(jnp.mean(values * values, axis=-1, keepdims=True) + EPSILON)


def halved_dot(left, right):
    return (
        bf16_dot(left[0], right[0], NN)
        + bf16_dot(left[1], right[0], NN)
        + bf16_dot(left[0], right[1], NN)
    )


def attend_block(mixed, at, out):
    lane = lax.broadcasted_iota(jnp.int32, (BLK, PAIR), 1)
    first = lane < HDIM
    zero = jnp.zeros((BLK, PAIR), jnp.bfloat16)
    ones = jnp.concatenate(
        [jnp.where(first, 1.0, 0.0), jnp.where(first, 0.0, 1.0)], axis=0
    ).astype(jnp.bfloat16)
    rows = pl.ds(at, BLK)
    for pair in range(HEADS // 2):
        start = pair * PAIR
        queries = mixed[rows, start : start + PAIR]
        keys = mixed[rows, D_T + start : D_T + start + PAIR]
        values = mixed[rows, 2 * D_T + start : 2 * D_T + start + PAIR]
        keys_two = jnp.concatenate(
            [jnp.where(first, keys, zero), jnp.where(first, zero, keys)], axis=0
        )
        values_two = jnp.concatenate(
            [jnp.where(first, values, zero), jnp.where(first, zero, values)], axis=0
        )
        scores = bf16_dot(queries, keys_two, NT)
        left, right = scores[:, :BLK], scores[:, BLK:]
        scale = HDIM ** (-0.5)
        left = jnp.exp((left - jnp.max(left, axis=1, keepdims=True)) * scale)
        right = jnp.exp((right - jnp.max(right, axis=1, keepdims=True)) * scale)
        weights = jnp.concatenate([left, right], axis=1).astype(jnp.bfloat16)
        summed = bf16_dot(weights, jnp.concatenate([values_two, ones], axis=1), NN)
        out[rows, start : start + PAIR] = (summed[:, :PAIR] / summed[:, PAIR:]).astype(jnp.bfloat16)


def shard_copies(plan, owners, target, semaphores, count):
    copies = []
    for i, (piece, start, rows, row) in enumerate(plan):
        at = pl.multiple_of(owners[i] * count + row, 16)
        copies.append(
            pltpu.make_async_copy(
                piece.at[pl.ds(start, rows)], target.at[pl.ds(at, rows)], semaphores.at[i]
            )
        )
    return copies


def place(device):
    student, pool = device // 8, device % 8
    return [student // 4, student // 2 % 2, student % 2, pool]


def moved(values, x=0, z=0, core=0):
    pairs = []
    for device in range(DEVICES):
        at = place(device)
        student = ((at[0] + x) % 4 * 2 + (at[1] ^ z)) * 2 + (at[2] ^ core)
        pairs.append((device, student * 8 + at[3]))
    return lax.ppermute(values, BOTH, pairs)


def with_core(pieces):
    return pieces + [moved(values, core=1) for values in pieces]


def shard_owners():
    x, z, core, _ = place(lax.axis_index("student") * 8)

    def index(dx, dz, dc):
        return (lax.rem(x + dx + 4, 4) * 2 + (z + dz) % 2) * 2 + (core + dc) % 2

    near = [index(dx, dz, dc) for dc in range(2) for dx in (0, -1, 1) for dz in range(2)]
    far = [index(2, dz, dc) for dc in range(2) for dz in range(2)]
    return jnp.stack(near + far).astype(jnp.int32)


def core_groups():
    groups = [[], []]
    for device in range(DEVICES):
        groups[(device // 8) % 2].append(device)
    return groups


def core_swap(values):
    pairs = [(d, d ^ 8) for d in range(DEVICES)]
    return lax.ppermute(values, BOTH, pairs)


def halves_of(values):
    high = lax.reduce_precision(values, 8, 7)
    return high.astype(jnp.bfloat16), (values - high).astype(jnp.bfloat16)


def cut(values):
    high = values.astype(jnp.bfloat16)
    return high, (values - high.astype(jnp.float32)).astype(jnp.bfloat16)


def three_parts(value, lane):
    first = value.astype(jnp.bfloat16).astype(jnp.float32)
    second = (value - first).astype(jnp.bfloat16).astype(jnp.float32)
    third = value - first - second
    row = jnp.where(lane == 0, first, jnp.where(lane == 1, second, third))
    return jnp.where(lane < 3, row, 0.0)


def dot_three(left, right, dims):
    at_left, at_right = dims[0][0][0], dims[0][1][0]
    wide = jnp.concatenate([left[0], left[1], left[0]], axis=at_left)
    other = jnp.concatenate([right[0], right[0], right[1]], axis=at_right)
    return bf16_dot(wide, other, dims)


def scale_of(values):
    return lax.rsqrt(jnp.mean(values * values, axis=1, keepdims=True) + EPSILON)


def hand_over(core, sums, mine, other, done):
    half = SUM_ROWS // 2
    at = pl.multiple_of(core * half, half)
    across = pl.multiple_of((1 - core) * half, half)
    copies = [
        pltpu.make_async_copy(sums.at[pl.ds(across, half)], other, done.at[0]),
        pltpu.make_async_copy(sums.at[pl.ds(at, half)], mine, done.at[1]),
    ]
    for copy in copies:
        copy.start()
    for copy in copies:
        copy.wait()


def project_rows(refs, owners, scopes):
    rows, gain, gathered, pieces, embedded, mixed, semaphores, others = refs
    embed, project, normed = scopes
    wide = D_T // 2
    first = [
        pltpu.make_async_copy(
            gathered.at[:, pl.ds(CUT, EMBED_PACK), pl.ds(i * wide, wide)], embed.at[:, i], others.at[i]
        )
        for i in range(2)
    ]
    for copy in first:
        copy.start()
    copies = [
        pltpu.make_async_copy(
            gathered.at[i, pl.ds(0, CUT)], project.at[pl.ds(i * P_ROWS, CUT)], others.at[2 + i]
        )
        for i in range(STUDENTS)
    ]
    plan = [(piece, 0, REST, CUT) for piece in pieces]
    copies += shard_copies(plan, owners, project, semaphores, P_ROWS)
    for copy in copies:
        copy.start()
    for copy in first:
        copy.wait()
    step = 2 * BLK

    @pl.loop(0, rows.shape[0] // step)
    def _(r):
        at = pl.ds(pl.multiple_of(r * step, step), step)
        weights = embed[...].reshape(D_T, wide)[:, :PIX_PAD]
        product = bf16_dot(rows[at, :], weights, NT)
        embedded[at, :] = product
        normed[at, :] = (product * scale_of(product) * gain[...]).astype(jnp.bfloat16)

    for copy in copies:
        copy.wait()
    tile = 512

    @pl.loop(0, 3 * D_T // tile)
    def _(n):
        at = pl.ds(pl.multiple_of(n * tile, tile), tile)
        mixed[:, at] = bf16_dot(normed[...], project[at, :], NT).astype(jnp.bfloat16)


def teacher_kernel(core, project_owners, output_owners, rows, gain, gathered, *rest):
    pieces, rest = rest[: NEAR + FAR], rest[NEAR + FAR :]
    high, rest = rest[:FAR], rest[FAR:]
    sources, rest = rest[:7], rest[7:]
    mine, other, down_rest, d_hidden_out, total, embedded, context, mixed, *semaphores = rest
    project_done, others, output_done, sources_done, done = semaphores
    count, block = rows.shape[0], 2 * BLK

    def project(*scopes):
        refs = rows, gain, gathered, pieces, embedded, mixed, project_done, others
        project_rows(refs, project_owners, scopes)

    pl.run_scoped(
        project,
        pltpu.VMEM((STUDENTS, 2, EMBED_PACK, D_T // 2), jnp.bfloat16),
        pltpu.VMEM((3 * D_T, D_T), jnp.bfloat16),
        pltpu.VMEM((count, D_T), jnp.bfloat16),
    )

    def compare(output, sums, *held):
        plan = [(piece, REST if i < NEAR else 0, O_ROWS, 0) for i, piece in enumerate(pieces[:NEAR] + high)]
        copies = shard_copies(plan, output_owners, output, output_done, O_ROWS)
        copies += [
            pltpu.make_async_copy(source, target, sources_done.at[i])
            for i, (source, target) in enumerate(zip(sources, held))
        ]
        for copy in copies:
            copy.start()
        sums[...] = jnp.zeros_like(sums)
        down_rest[...] = jnp.zeros_like(down_rest)
        total[...] = jnp.zeros_like(total)

        @pl.loop(0, count // BLK)
        def _(b):
            attend_block(mixed, pl.multiple_of(b * BLK, BLK), context)

        for copy in copies:
            copy.wait()
        student_out, hidden_hi, hidden_lo, act_hi, act_lo, head_hi, head_lo = held

        @pl.loop(0, count // block)
        def _(r):
            at = pl.ds(pl.multiple_of(r * block, block), block)
            finished = embedded[at, :] + bf16_dot(context[at, :], output[...], NT)
            features = (finished * scale_of(finished)).astype(jnp.bfloat16).astype(jnp.float32)
            out = student_out[at, :]
            dot_mean = jnp.mean(out * features, axis=1, keepdims=True)
            out_scale, feature_scale = scale_of(out), scale_of(features)
            both = out_scale * feature_scale
            total[...] += jnp.sum(dot_mean * both)
            along = both * (-1.0 / D_T)
            back = both * dot_mean * out_scale * out_scale * (1.0 / D_T)
            d_out = cut(along * features + back * out)
            grad_head = dot_three((hidden_hi[at, :], hidden_lo[at, :]), d_out, TN)
            for i in range(D_T // LANES):
                sums[i * D_S : (i + 1) * D_S, :] += grad_head[:, i * LANES : (i + 1) * LANES]
            d_hidden = dot_three(d_out, (head_hi[...], head_lo[...]), NT)
            d_hidden_out[at, :] = d_hidden
            grad_down = dot_three((act_hi[at, :], act_lo[at, :]), cut(d_hidden), TN)
            start = D_S * D_T // LANES
            for i in range(2):
                columns = slice(i * LANES, (i + 1) * LANES)
                sums[start + i * S_HID : start + (i + 1) * S_HID, :] += grad_down[:, columns]
            down_rest[...] += grad_down[:, 2 * LANES :]

        hand_over(core[0], sums, mine, other, done)

    pl.run_scoped(
        compare,
        pltpu.VMEM((D_T, D_T), jnp.bfloat16),
        pltpu.VMEM((SUM_ROWS, LANES), jnp.float32),
        *[pltpu.VMEM(source.shape, source.dtype) for source in sources],
    )


def teacher_and_head(core, owners, rows, gain, gathered, pieces, high, student_out, hidden, act, head):
    count = rows.shape[0]
    smem, vmem, anywhere = [
        pl.BlockSpec(memory_space=space) for space in (pltpu.SMEM, pltpu.VMEM, pl.ANY)
    ]
    sources = (student_out, *hidden, *act, *head)
    return pl.pallas_call(
        teacher_kernel,
        in_specs=[smem] * 3 + [vmem] * 2 + [anywhere] * (1 + len(pieces) + len(high) + len(sources)),
        out_specs=[anywhere] * 2 + [vmem] * 3,
        out_shape=[
            jax.ShapeDtypeStruct((SUM_ROWS // 2, LANES), jnp.float32),
            jax.ShapeDtypeStruct((SUM_ROWS // 2, LANES), jnp.float32),
            jax.ShapeDtypeStruct((S_HID, LANES), jnp.float32),
            jax.ShapeDtypeStruct((count, D_S), jnp.float32),
            jax.ShapeDtypeStruct((8, LANES), jnp.float32),
        ],
        scratch_shapes=[
            pltpu.VMEM((count, D_T), jnp.float32),
            pltpu.VMEM((count, D_T), jnp.bfloat16),
            pltpu.VMEM((count, 3 * D_T), jnp.bfloat16),
            pltpu.SemaphoreType.DMA((NEAR + FAR,)),
            pltpu.SemaphoreType.DMA((2 + STUDENTS,)),
            pltpu.SemaphoreType.DMA((NEAR + FAR,)),
            pltpu.SemaphoreType.DMA((len(sources),)),
            pltpu.SemaphoreType.DMA((2,)),
        ],
        compiler_params=pltpu.CompilerParams(vmem_limit_bytes=60 * 1024 * 1024),
        cost_estimate=pl.CostEstimate(
            flops=2 * count * D_T * (PIX_PAD + 4 * D_T + 9 * D_S),
            bytes_accessed=50 * 1024 * 1024,
            transcendentals=0,
        ),
        name="teacher_and_head",
    )(core, owners, owners, rows, gain, gathered, *pieces, *high, *sources)


def trunk_kernel(
    core, d_hidden, slope, down_hi, down_lo, up_hi, up_lo, normed_hi, normed_lo, lifted, gain, rows,
    down_rest, total, mine, other, sums, dh_hi, dh_lo, d_normed, done,
):
    step = pl.program_id(0)
    tile = slope.shape[1]

    @pl.when(step == 0)
    def _():
        dh_hi[...], dh_lo[...] = cut(d_hidden[...])
        d_normed[...] = jnp.zeros_like(d_normed)
        sums[:UP_AT, :] = down_rest[...]
        sums[GAIN_AT:, :] = jnp.zeros((SUM_ROWS - GAIN_AT, LANES), jnp.float32)

    d_act = dot_three((dh_hi[...], dh_lo[...]), (down_hi[...], down_lo[...]), NT)
    d_pre = cut(d_act * slope[...])
    grad_up = dot_three((normed_hi[...], normed_lo[...]), d_pre, TN)
    at = pl.multiple_of(UP_AT + step * (tile // LANES) * D_S, LANES)
    for i in range(tile // LANES):
        sums[pl.ds(at + i * D_S, D_S), :] = grad_up[:, i * LANES : (i + 1) * LANES]
    d_normed[...] += dot_three(d_pre, (up_hi[...], up_lo[...]), NT)

    @pl.when(step == pl.num_programs(0) - 1)
    def _():
        d_out = d_normed[...]
        scale = scale_of(lifted[...])
        across = lifted[...] * scale
        grad_gain = jnp.sum(d_out * across, axis=0, keepdims=True)
        d_unit = d_out * gain[...]
        inner = jnp.mean(d_unit * across, axis=1, keepdims=True)
        d_lifted = cut(d_hidden[...] + scale * (d_unit - across * inner))
        grad_embed = bf16_dot(rows[...], d_lifted[0], TN) + bf16_dot(rows[...], d_lifted[1], TN)
        for i in range(D_S // LANES):
            columns = slice(i * LANES, (i + 1) * LANES)
            start = EMBED_AT + i * EMBED_ROWS
            sums[start : start + EMBED_ROWS, :] = grad_embed[:EMBED_ROWS, columns]
            sums[GAIN_AT + i : GAIN_AT + i + 1, :] = grad_gain[:, columns]
        lane = lax.broadcasted_iota(jnp.int32, (1, LANES), 1)
        sums[SUM_ROWS - 1 :, :] = three_parts(total[0:1, :], lane)
        hand_over(core[0], sums, mine, other, done)


def trunk_backward(core, d_hidden, slope, down, up, normed, lifted, gain, rows, down_rest, total):
    count = d_hidden.shape[0]
    tile = 512

    def whole(values):
        return pl.BlockSpec(values.shape, lambda j: (0, 0))

    down_spec = pl.BlockSpec((tile, D_S), lambda j: (j, 0))
    up_spec = pl.BlockSpec((D_S, tile), lambda j: (0, j))
    return pl.pallas_call(
        trunk_kernel,
        grid=(S_HID // tile,),
        in_specs=[
            pl.BlockSpec(memory_space=pltpu.SMEM),
            whole(d_hidden), pl.BlockSpec((count, tile), lambda j: (0, j)),
            down_spec, down_spec, up_spec, up_spec,
            whole(normed[0]), whole(normed[1]), whole(lifted), whole(gain), whole(rows),
            whole(down_rest), whole(total),
        ],
        out_specs=[pl.BlockSpec(memory_space=pl.ANY)] * 2,
        out_shape=[jax.ShapeDtypeStruct((SUM_ROWS // 2, LANES), jnp.float32)] * 2,
        scratch_shapes=[
            pltpu.VMEM((SUM_ROWS, LANES), jnp.float32),
            pltpu.VMEM((count, D_S), jnp.bfloat16),
            pltpu.VMEM((count, D_S), jnp.bfloat16),
            pltpu.VMEM((count, D_S), jnp.float32),
            pltpu.SemaphoreType.DMA((2,)),
        ],
        compiler_params=pltpu.CompilerParams(vmem_limit_bytes=56 * 1024 * 1024),
        cost_estimate=pl.CostEstimate(
            flops=2 * count * D_S * (9 * S_HID + 2 * PIX_PAD), bytes_accessed=30 * 1024 * 1024, transcendentals=0
        ),
        name="trunk_backward",
    )(core, d_hidden, slope, *down, *up, *normed, lifted, gain, rows, down_rest, total)


def unpack_kernel(
    core, mine_hbm, theirs_hbm, head_hbm, down_hbm, up_hbm, embed_hbm, gain, mean_distance,
    mine, theirs, head, down, up, embed, semaphores,
):
    arrivals = [
        pltpu.make_async_copy(mine_hbm, mine, semaphores.at[0]),
        pltpu.make_async_copy(theirs_hbm, theirs, semaphores.at[1]),
    ]
    results = [
        pltpu.make_async_copy(source, target, semaphores.at[2 + i])
        for i, (source, target) in enumerate(
            [(head, head_hbm), (down, down_hbm), (up, up_hbm), (embed, embed_hbm)]
        )
    ]
    for copy in arrivals:
        copy.start()
    for copy in arrivals:
        copy.wait()

    def take(halves, part, start, count):
        pieces, stop = [], start + count
        while start < stop:
            rank, row = start // CHUNK, start % CHUNK
            size = min(CHUNK - row, stop - start)
            at = part * CHUNK + row
            pieces.append(halves[rank // RANKS][rank % RANKS, at : at + size, :].astype(jnp.float32))
            start += size
        return pieces[0] if len(pieces) == 1 else jnp.concatenate(pieces, axis=0)

    def strip(i):
        return slice(i * LANES, (i + 1) * LANES)

    def unpack_head(halves):
        for i in range(D_T // LANES):
            head[:, strip(i)] = take(halves, 0, i * D_S, D_S)

    def unpack_down(halves):
        at = D_S * D_T // LANES
        for i in range(2):
            down[:, strip(i)] = take(halves, 0, at + i * S_HID, S_HID)
        down[:, 2 * LANES :] = take(halves, 1, 0, S_HID)

    def unpack_up(halves):
        for i in range(S_HID // LANES):
            up[:, strip(i)] = take(halves, 1, UP_AT + i * D_S, D_S)

    def unpack_rest(halves):
        for i in range(D_S // LANES):
            embed[:, strip(i)] = take(halves, 1, EMBED_AT + i * EMBED_ROWS, EMBED_ROWS)[:PIX]
        gains = take(halves, 1, GAIN_AT, 16)
        for i in range(D_S // LANES):
            gain[strip(i)] = gains[i]
        lane = lax.broadcasted_iota(jnp.int32, (1, LANES), 1)
        cosines = jnp.where(lane < 3, take(halves, 1, SUM_ROWS - 16, 16)[15:], 0.0)
        mean_distance[0] = 1.0 - jnp.sum(cosines) * (1.0 / (DEVICES * 2 * BLK))

    for unpack, copy in zip([unpack_head, unpack_down, unpack_up, unpack_rest], results):

        @pl.when(core[0] == 0)
        def _():
            unpack((mine, theirs))

        @pl.when(core[0] == 1)
        def _():
            unpack((theirs, mine))

        copy.start()
    for copy in results:
        copy.wait()


def unpack_sums(core, mine, theirs):
    smem, vmem, anywhere = [
        pl.BlockSpec(memory_space=space) for space in (pltpu.SMEM, pltpu.VMEM, pl.ANY)
    ]
    shapes = [(D_S, D_T), (S_HID, D_S), (D_S, S_HID), (PIX, D_S)]
    return pl.pallas_call(
        unpack_kernel,
        in_specs=[smem, anywhere, anywhere],
        out_specs=[anywhere] * 4 + [vmem, smem],
        out_shape=[jax.ShapeDtypeStruct(shape, jnp.float32) for shape in shapes + [(D_S,), (1,)]],
        scratch_shapes=[pltpu.VMEM(mine.shape, mine.dtype)] * 2
        + [pltpu.VMEM(shape, jnp.float32) for shape in shapes]
        + [pltpu.SemaphoreType.DMA((6,))],
        compiler_params=pltpu.CompilerParams(vmem_limit_bytes=24 * 1024 * 1024),
        cost_estimate=pl.CostEstimate(flops=0, bytes_accessed=12 * 1024 * 1024, transcendentals=0),
        name="unpack_sums",
    )(core, mine, theirs)


def core_sum(mine, theirs):
    return (mine + theirs).astype(jnp.bfloat16).reshape(RANKS, CHUNK, LANES)


def to_all_ranks(values):
    return lax.all_to_all(values, BOTH, 0, 0, axis_index_groups=core_groups(), tiled=True)


def chunk_kernel(owner, got, spread):
    chunk = jnp.sum(got[...].astype(jnp.float32), axis=0)
    lane = lax.broadcasted_iota(jnp.int32, (1, LANES), 1)
    parts = chunk[2 * CHUNK - 1 :, :]
    whole = jnp.sum(jnp.where(lane < 3, parts, 0.0), axis=1, keepdims=True)
    last = jnp.where(owner[0] == 1, three_parts(whole, lane), parts)
    rounded = jnp.concatenate([chunk[: 2 * CHUNK - 1, :], last], axis=0).astype(jnp.bfloat16)
    spread[...] = jnp.broadcast_to(rounded[None], spread.shape)


def add_chunk(owner, got):
    vmem = pl.BlockSpec(memory_space=pltpu.VMEM)
    return pl.pallas_call(
        chunk_kernel,
        in_specs=[pl.BlockSpec(memory_space=pltpu.SMEM), vmem],
        out_specs=vmem,
        out_shape=jax.ShapeDtypeStruct(got.shape, jnp.bfloat16),
        compiler_params=pltpu.CompilerParams(vmem_limit_bytes=32 * 1024 * 1024),
        cost_estimate=pl.CostEstimate(flops=0, bytes_accessed=4 * 1024 * 1024, transcendentals=0),
        name="add_chunk",
    )(owner, got)


def on_device(
    pixels,
    keyframes,
    destination,
    student_embed,
    student_gain,
    student_up,
    student_down,
    student_head,
    teacher_embed,
    teacher_gain,
    teacher_project,
    teacher_output,
):
    pool_size = lax.axis_size("pool")

    project = teacher_project[0].T
    embed_shard = jnp.pad(teacher_embed[0].T, ((0, 0), (0, D_T // 2 - PIX)))
    embed_shard = jnp.concatenate([embed_shard[:EMBED_PACK], embed_shard[EMBED_PACK:]], axis=1)
    gathered = lax.all_gather(
        jnp.concatenate([project[:CUT], embed_shard], axis=0), "student", axis=0, tiled=False
    )
    shard = jnp.concatenate([project[CUT:], teacher_output[0].T], axis=0)
    first = [moved(shard, z=1), moved(shard, x=1), moved(shard, x=-1)]

    owners = shard_owners()

    teachers = jnp.arange(pool_size, dtype=jnp.int32)[:, None, None]
    chosen = [
        lax.dynamic_index_in_dim(pixels, keyframes[0, k], 0, keepdims=True) for k in range(2)
    ]
    outgoing = jnp.where(
        destination[0, 0] == teachers,
        chosen[0],
        jnp.where(destination[0, 1] == teachers, chosen[1], jnp.zeros((), jnp.bfloat16)),
    )
    outgoing = jnp.pad(outgoing, ((0, 0), (0, 0), (0, PIX_PAD - PIX)))
    up, down, head = halves_of(student_up), halves_of(student_down), halves_of(student_head)
    embed = halves_of(jnp.pad(student_embed, ((0, PIX_PAD - PIX), (0, 0))))
    outgoing, up, down, head, embed, gain, *first = lax.optimization_barrier(
        (outgoing, up, down, head, embed, student_gain[None], *first)
    )
    across, back, ahead = first
    second = [
        moved(across, x=1), moved(across, x=-1), moved(back[:REST], x=1), moved(ahead[REST:], x=-1)
    ]
    arrived = lax.all_to_all(outgoing, "pool", split_axis=0, concat_axis=0, tiled=True)
    rows = arrived.reshape(pool_size * BLK, PIX_PAD)

    lifted = bf16_dot(rows, embed[0], NN) + bf16_dot(rows, embed[1], NN)
    normed_s = halves_of(lifted * rms_scale(lifted) * student_gain)
    pre = halved_dot(normed_s, up)
    cdf = 0.5 * (1.0 + lax.erf(pre * (2.0**-0.5)))
    act = halves_of(pre * cdf)
    slope = cdf + pre * jnp.exp(-0.5 * pre * pre) * ((2.0 * jnp.pi) ** -0.5)
    act, slope, *second = lax.optimization_barrier((act, slope, *second))
    back_across, ahead_across, low_near, high_near = second
    third = [moved(back_across[:REST], x=1), moved(ahead_across[REST:], x=-1)]
    near = with_core([shard, across, back, back_across, ahead, ahead_across])
    hidden = halves_of(lifted + halved_dot(act, down))
    student_out = halved_dot(hidden, head)
    student_out, *third = lax.optimization_barrier((student_out, *third))
    low = with_core([low_near, third[0]])
    high = with_core([high_near, third[1]])

    core = lax.rem(lax.axis_index("student"), 2).reshape(1)
    *sums_a, down_rest, d_hidden, total = teacher_and_head(
        core, owners, rows, teacher_gain, gathered, near + low, high, student_out, hidden, act, head
    )
    theirs_a = core_swap(sums_a[1])
    sums_b = trunk_backward(
        core, d_hidden, slope, down, up, normed_s, lifted, gain, rows, down_rest, total
    )
    rank = lax.axis_index("student") // 2 * 8 + lax.axis_index("pool")
    owner = jnp.logical_and(core == 1, rank == RANKS - 1).astype(jnp.int32)
    theirs_a, *sums_b = lax.optimization_barrier((theirs_a, *sums_b))
    sent = [core_sum(sums_a[0], theirs_a), core_sum(sums_b[0], core_swap(sums_b[1]))]
    got = to_all_ranks(jnp.concatenate(sent, axis=1))
    half = to_all_ranks(add_chunk(owner, got))
    head_sum, down_sum, up_sum, embed_sum, gain_sum, mean_distance = unpack_sums(
        core, half, core_swap(half)
    )
    return (mean_distance.reshape(()), embed_sum, gain_sum, up_sum, down_sum, head_sum)


def solution(mesh):
    in_specs = (
        P(("student", "pool"), None, None),
        P(("student", "pool"), None),
        P(("student", "pool"), None),
        P(),
        P(),
        P(),
        P(),
        P(),
        P("pool", None, "student"),
        P("pool", None),
        P("pool", None, "student"),
        P("pool", None, "student"),
    )
    out_specs = (P(), P(), P(), P(), P(), P())
    return jax.shard_map(
        on_device, mesh=mesh, in_specs=in_specs, out_specs=out_specs, check_vma=False
    )
```

```python
import jax
import jax.numpy as jnp
from jax import lax
from jax.experimental import pallas as pl
from jax.experimental.pallas import tpu as pltpu
from jax.sharding import PartitionSpec as P

HEADS = 24
HDIM = 64
EPSILON = 1e-06
BOTH = ("student", "pool")
DEVICES = 128
PAIR = 2 * HDIM
LANES = 128
PIX = 588
PIX_PAD = 640
D_S = 384
D_T = 1536
S_HID = 1536
BLK = 128
P_ROWS = 288
O_ROWS = 96
NEAR = 12
FAR = 4
CUT = 208
REST = P_ROWS - CUT
STUDENTS = 16
EMBED_PACK = 48
RANKS = DEVICES // 2
CHUNK = 64
SUM_ROWS = 2 * RANKS * CHUNK
EMBED_ROWS = 592
UP_AT = S_HID
EMBED_AT = UP_AT + D_S * S_HID // LANES
GAIN_AT = EMBED_AT + (D_S // LANES) * EMBED_ROWS
NT = (((1,), (1,)), ((), ()))
TN = (((0,), (0,)), ((), ()))
NN = (((1,), (0,)), ((), ()))


def bf16_dot(left, right, dims):
    return lax.dot_general(left, right, dims, preferred_element_type=jnp.float32)


def rms_scale(values):
    return lax.rsqrt(jnp.mean(values * values, axis=-1, keepdims=True) + EPSILON)


def halved_dot(left, right):
    return (
        bf16_dot(left[0], right[0], NN)
        + bf16_dot(left[1], right[0], NN)
        + bf16_dot(left[0], right[1], NN)
    )


def attend_block(mixed, at, out):
    lane = lax.broadcasted_iota(jnp.int32, (BLK, PAIR), 1)
    first = lane < HDIM
    zero = jnp.zeros((BLK, PAIR), jnp.bfloat16)
    ones = jnp.concatenate(
        [jnp.where(first, 1.0, 0.0), jnp.where(first, 0.0, 1.0)], axis=0
    ).astype(jnp.bfloat16)
    rows = pl.ds(at, BLK)
    for pair in range(HEADS // 2):
        start = pair * PAIR
        queries = mixed[rows, start : start + PAIR]
        keys = mixed[rows, D_T + start : D_T + start + PAIR]
        values = mixed[rows, 2 * D_T + start : 2 * D_T + start + PAIR]
        keys_two = jnp.concatenate(
            [jnp.where(first, keys, zero), jnp.where(first, zero, keys)], axis=0
        )
        values_two = jnp.concatenate(
            [jnp.where(first, values, zero), jnp.where(first, zero, values)], axis=0
        )
        scores = bf16_dot(queries, keys_two, NT)
        left, right = scores[:, :BLK], scores[:, BLK:]
        scale = HDIM ** (-0.5)
        left = jnp.exp((left - jnp.max(left, axis=1, keepdims=True)) * scale)
        right = jnp.exp((right - jnp.max(right, axis=1, keepdims=True)) * scale)
        weights = jnp.concatenate([left, right], axis=1).astype(jnp.bfloat16)
        summed = bf16_dot(weights, jnp.concatenate([values_two, ones], axis=1), NN)
        out[rows, start : start + PAIR] = (summed[:, :PAIR] / summed[:, PAIR:]).astype(jnp.bfloat16)


def shard_copies(plan, owners, target, semaphores, count):
    copies = []
    for i, (piece, start, rows, row) in enumerate(plan):
        at = pl.multiple_of(owners[i] * count + row, 16)
        copies.append(
            pltpu.make_async_copy(
                piece.at[pl.ds(start, rows)], target.at[pl.ds(at, rows)], semaphores.at[i]
            )
        )
    return copies


def place(device):
    student, pool = device // 8, device % 8
    return [student // 4, student // 2 % 2, student % 2, pool]


def moved(values, x=0, z=0, core=0):
    pairs = []
    for device in range(DEVICES):
        at = place(device)
        student = ((at[0] + x) % 4 * 2 + (at[1] ^ z)) * 2 + (at[2] ^ core)
        pairs.append((device, student * 8 + at[3]))
    return lax.ppermute(values, BOTH, pairs)


def with_core(pieces):
    return pieces + [moved(values, core=1) for values in pieces]


def shard_owners():
    x, z, core, _ = place(lax.axis_index("student") * 8)

    def index(dx, dz, dc):
        return (lax.rem(x + dx + 4, 4) * 2 + (z + dz) % 2) * 2 + (core + dc) % 2

    near = [index(dx, dz, dc) for dc in range(2) for dx in (0, -1, 1) for dz in range(2)]
    far = [index(2, dz, dc) for dc in range(2) for dz in range(2)]
    return jnp.stack(near + far).astype(jnp.int32)


def core_groups():
    groups = [[], []]
    for device in range(DEVICES):
        groups[(device // 8) % 2].append(device)
    return groups


def core_swap(values):
    pairs = [(d, d ^ 8) for d in range(DEVICES)]
    return lax.ppermute(values, BOTH, pairs)


def halves_of(values):
    high = lax.reduce_precision(values, 8, 7)
    return high.astype(jnp.bfloat16), (values - high).astype(jnp.bfloat16)


def cut(values):
    high = values.astype(jnp.bfloat16)
    return high, (values - high.astype(jnp.float32)).astype(jnp.bfloat16)


def three_parts(value, lane):
    first = value.astype(jnp.bfloat16).astype(jnp.float32)
    second = (value - first).astype(jnp.bfloat16).astype(jnp.float32)
    third = value - first - second
    row = jnp.where(lane == 0, first, jnp.where(lane == 1, second, third))
    return jnp.where(lane < 3, row, 0.0)


def dot_three(left, right, dims):
    at_left, at_right = dims[0][0][0], dims[0][1][0]
    wide = jnp.concatenate([left[0], left[1], left[0]], axis=at_left)
    other = jnp.concatenate([right[0], right[0], right[1]], axis=at_right)
    return bf16_dot(wide, other, dims)


def scale_of(values):
    return lax.rsqrt(jnp.mean(values * values, axis=1, keepdims=True) + EPSILON)


def hand_over(core, sums, mine, other, done):
    half = SUM_ROWS // 2
    at = pl.multiple_of(core * half, half)
    across = pl.multiple_of((1 - core) * half, half)
    copies = [
        pltpu.make_async_copy(sums.at[pl.ds(across, half)], other, done.at[0]),
        pltpu.make_async_copy(sums.at[pl.ds(at, half)], mine, done.at[1]),
    ]
    for copy in copies:
        copy.start()
    for copy in copies:
        copy.wait()


def project_rows(refs, owners, scopes):
    rows, gain, gathered, pieces, embedded, mixed, semaphores, others = refs
    embed, project, normed = scopes
    wide = D_T // 2
    first = [
        pltpu.make_async_copy(
            gathered.at[:, pl.ds(CUT, EMBED_PACK), pl.ds(i * wide, wide)], embed.at[:, i], others.at[i]
        )
        for i in range(2)
    ]
    for copy in first:
        copy.start()
    copies = [
        pltpu.make_async_copy(
            gathered.at[i, pl.ds(0, CUT)], project.at[pl.ds(i * P_ROWS, CUT)], others.at[2 + i]
        )
        for i in range(STUDENTS)
    ]
    plan = [(piece, 0, REST, CUT) for piece in pieces]
    copies += shard_copies(plan, owners, project, semaphores, P_ROWS)
    for copy in copies:
        copy.start()
    for copy in first:
        copy.wait()
    step = 4 * BLK

    @pl.loop(0, rows.shape[0] // step)
    def _(r):
        at = pl.ds(pl.multiple_of(r * step, step), step)
        weights = embed[...].reshape(D_T, wide)[:, :PIX_PAD]
        product = bf16_dot(rows[at, :], weights, NT)
        embedded[at, :] = product
        normed[at, :] = (product * scale_of(product) * gain[...]).astype(jnp.bfloat16)

    for copy in copies:
        copy.wait()
    tile = 1536

    @pl.loop(0, 3 * D_T // tile)
    def _(n):
        at = pl.ds(pl.multiple_of(n * tile, tile), tile)
        mixed[:, at] = bf16_dot(normed[...], project[at, :], NT).astype(jnp.bfloat16)


def teacher_kernel(core, project_owners, output_owners, rows, gain, gathered, *rest):
    pieces, rest = rest[: NEAR + FAR], rest[NEAR + FAR :]
    high, rest = rest[:FAR], rest[FAR:]
    sources, rest = rest[:7], rest[7:]
    mine, other, down_rest, d_hidden_out, total, embedded, context, mixed, *semaphores = rest
    project_done, others, output_done, sources_done, done = semaphores
    count, block = rows.shape[0], 2 * BLK

    def project(*scopes):
        refs = rows, gain, gathered, pieces, embedded, mixed, project_done, others
        project_rows(refs, project_owners, scopes)

    pl.run_scoped(
        project,
        pltpu.VMEM((STUDENTS, 2, EMBED_PACK, D_T // 2), jnp.bfloat16),
        pltpu.VMEM((3 * D_T, D_T), jnp.bfloat16),
        pltpu.VMEM((count, D_T), jnp.bfloat16),
    )

    def compare(output, sums, *held):
        plan = [(piece, REST if i < NEAR else 0, O_ROWS, 0) for i, piece in enumerate(pieces[:NEAR] + high)]
        copies = shard_copies(plan, output_owners, output, output_done, O_ROWS)
        copies += [
            pltpu.make_async_copy(source, target, sources_done.at[i])
            for i, (source, target) in enumerate(zip(sources, held))
        ]
        for copy in copies:
            copy.start()
        sums[...] = jnp.zeros_like(sums)
        down_rest[...] = jnp.zeros_like(down_rest)
        total[...] = jnp.zeros_like(total)

        @pl.loop(0, count // BLK)
        def _(b):
            attend_block(mixed, pl.multiple_of(b * BLK, BLK), context)

        for copy in copies:
            copy.wait()
        student_out, hidden_hi, hidden_lo, act_hi, act_lo, head_hi, head_lo = held

        @pl.loop(0, count // block)
        def _(r):
            at = pl.ds(pl.multiple_of(r * block, block), block)
            finished = embedded[at, :] + bf16_dot(context[at, :], output[...], NT)
            features = (finished * scale_of(finished)).astype(jnp.bfloat16).astype(jnp.float32)
            out = student_out[at, :]
            dot_mean = jnp.mean(out * features, axis=1, keepdims=True)
            out_scale, feature_scale = scale_of(out), scale_of(features)
            both = out_scale * feature_scale
            total[...] += jnp.sum(dot_mean * both)
            along = both * (-1.0 / D_T)
            back = both * dot_mean * out_scale * out_scale * (1.0 / D_T)
            d_out = cut(along * features + back * out)
            grad_head = dot_three((hidden_hi[at, :], hidden_lo[at, :]), d_out, TN)
            for i in range(D_T // LANES):
                sums[i * D_S : (i + 1) * D_S, :] += grad_head[:, i * LANES : (i + 1) * LANES]
            d_hidden = dot_three(d_out, (head_hi[...], head_lo[...]), NT)
            d_hidden_out[at, :] = d_hidden
            grad_down = dot_three((act_hi[at, :], act_lo[at, :]), cut(d_hidden), TN)
            start = D_S * D_T // LANES
            for i in range(2):
                columns = slice(i * LANES, (i + 1) * LANES)
                sums[start + i * S_HID : start + (i + 1) * S_HID, :] += grad_down[:, columns]
            down_rest[...] += grad_down[:, 2 * LANES :]

        hand_over(core[0], sums, mine, other, done)

    pl.run_scoped(
        compare,
        pltpu.VMEM((D_T, D_T), jnp.bfloat16),
        pltpu.VMEM((SUM_ROWS, LANES), jnp.float32),
        *[pltpu.VMEM(source.shape, source.dtype) for source in sources],
    )


def teacher_and_head(core, owners, rows, gain, gathered, pieces, high, student_out, hidden, act, head):
    count = rows.shape[0]
    smem, vmem, anywhere = [
        pl.BlockSpec(memory_space=space) for space in (pltpu.SMEM, pltpu.VMEM, pl.ANY)
    ]
    sources = (student_out, *hidden, *act, *head)
    return pl.pallas_call(
        teacher_kernel,
        in_specs=[smem] * 3 + [vmem] * 2 + [anywhere] * (1 + len(pieces) + len(high) + len(sources)),
        out_specs=[anywhere] * 2 + [vmem] * 3,
        out_shape=[
            jax.ShapeDtypeStruct((SUM_ROWS // 2, LANES), jnp.float32),
            jax.ShapeDtypeStruct((SUM_ROWS // 2, LANES), jnp.float32),
            jax.ShapeDtypeStruct((S_HID, LANES), jnp.float32),
            jax.ShapeDtypeStruct((count, D_S), jnp.float32),
            jax.ShapeDtypeStruct((8, LANES), jnp.float32),
        ],
        scratch_shapes=[
            pltpu.VMEM((count, D_T), jnp.float32),
            pltpu.VMEM((count, D_T), jnp.bfloat16),
            pltpu.VMEM((count, 3 * D_T), jnp.bfloat16),
            pltpu.SemaphoreType.DMA((NEAR + FAR,)),
            pltpu.SemaphoreType.DMA((2 + STUDENTS,)),
            pltpu.SemaphoreType.DMA((NEAR + FAR,)),
            pltpu.SemaphoreType.DMA((len(sources),)),
            pltpu.SemaphoreType.DMA((2,)),
        ],
        compiler_params=pltpu.CompilerParams(vmem_limit_bytes=60 * 1024 * 1024),
        cost_estimate=pl.CostEstimate(
            flops=2 * count * D_T * (PIX_PAD + 4 * D_T + 9 * D_S),
            bytes_accessed=50 * 1024 * 1024,
            transcendentals=0,
        ),
        name="teacher_and_head",
    )(core, owners, owners, rows, gain, gathered, *pieces, *high, *sources)


def trunk_kernel(
    core, d_hidden, slope, down_hi, down_lo, up_hi, up_lo, normed_hi, normed_lo, lifted, gain, rows,
    down_rest, total, mine, other, sums, dh_hi, dh_lo, d_normed, done,
):
    step = pl.program_id(0)
    tile = slope.shape[1]

    @pl.when(step == 0)
    def _():
        dh_hi[...], dh_lo[...] = cut(d_hidden[...])
        d_normed[...] = jnp.zeros_like(d_normed)
        sums[:UP_AT, :] = down_rest[...]
        sums[GAIN_AT:, :] = jnp.zeros((SUM_ROWS - GAIN_AT, LANES), jnp.float32)

    d_act = dot_three((dh_hi[...], dh_lo[...]), (down_hi[...], down_lo[...]), NT)
    d_pre = cut(d_act * slope[...])
    grad_up = dot_three((normed_hi[...], normed_lo[...]), d_pre, TN)
    at = pl.multiple_of(UP_AT + step * (tile // LANES) * D_S, LANES)
    for i in range(tile // LANES):
        sums[pl.ds(at + i * D_S, D_S), :] = grad_up[:, i * LANES : (i + 1) * LANES]
    d_normed[...] += dot_three(d_pre, (up_hi[...], up_lo[...]), NT)

    @pl.when(step == pl.num_programs(0) - 1)
    def _():
        d_out = d_normed[...]
        scale = scale_of(lifted[...])
        across = lifted[...] * scale
        grad_gain = jnp.sum(d_out * across, axis=0, keepdims=True)
        d_unit = d_out * gain[...]
        inner = jnp.mean(d_unit * across, axis=1, keepdims=True)
        d_lifted = cut(d_hidden[...] + scale * (d_unit - across * inner))
        grad_embed = bf16_dot(rows[...], d_lifted[0], TN) + bf16_dot(rows[...], d_lifted[1], TN)
        for i in range(D_S // LANES):
            columns = slice(i * LANES, (i + 1) * LANES)
            start = EMBED_AT + i * EMBED_ROWS
            sums[start : start + EMBED_ROWS, :] = grad_embed[:EMBED_ROWS, columns]
            sums[GAIN_AT + i : GAIN_AT + i + 1, :] = grad_gain[:, columns]
        lane = lax.broadcasted_iota(jnp.int32, (1, LANES), 1)
        sums[SUM_ROWS - 1 :, :] = three_parts(total[0:1, :], lane)
        hand_over(core[0], sums, mine, other, done)


def trunk_backward(core, d_hidden, slope, down, up, normed, lifted, gain, rows, down_rest, total):
    count = d_hidden.shape[0]
    tile = 512

    def whole(values):
        return pl.BlockSpec(values.shape, lambda j: (0, 0))

    down_spec = pl.BlockSpec((tile, D_S), lambda j: (j, 0))
    up_spec = pl.BlockSpec((D_S, tile), lambda j: (0, j))
    return pl.pallas_call(
        trunk_kernel,
        grid=(S_HID // tile,),
        in_specs=[
            pl.BlockSpec(memory_space=pltpu.SMEM),
            whole(d_hidden), pl.BlockSpec((count, tile), lambda j: (0, j)),
            down_spec, down_spec, up_spec, up_spec,
            whole(normed[0]), whole(normed[1]), whole(lifted), whole(gain), whole(rows),
            whole(down_rest), whole(total),
        ],
        out_specs=[pl.BlockSpec(memory_space=pl.ANY)] * 2,
        out_shape=[jax.ShapeDtypeStruct((SUM_ROWS // 2, LANES), jnp.float32)] * 2,
        scratch_shapes=[
            pltpu.VMEM((SUM_ROWS, LANES), jnp.float32),
            pltpu.VMEM((count, D_S), jnp.bfloat16),
            pltpu.VMEM((count, D_S), jnp.bfloat16),
            pltpu.VMEM((count, D_S), jnp.float32),
            pltpu.SemaphoreType.DMA((2,)),
        ],
        compiler_params=pltpu.CompilerParams(vmem_limit_bytes=56 * 1024 * 1024),
        cost_estimate=pl.CostEstimate(
            flops=2 * count * D_S * (9 * S_HID + 2 * PIX_PAD), bytes_accessed=30 * 1024 * 1024, transcendentals=0
        ),
        name="trunk_backward",
    )(core, d_hidden, slope, *down, *up, *normed, lifted, gain, rows, down_rest, total)


def unpack_kernel(
    core, mine_hbm, theirs_hbm, head_hbm, down_hbm, up_hbm, embed_hbm, gain, mean_distance,
    mine, theirs, head, down, up, embed, semaphores,
):
    arrivals = [
        pltpu.make_async_copy(mine_hbm, mine, semaphores.at[0]),
        pltpu.make_async_copy(theirs_hbm, theirs, semaphores.at[1]),
    ]
    results = [
        pltpu.make_async_copy(source, target, semaphores.at[2 + i])
        for i, (source, target) in enumerate(
            [(head, head_hbm), (down, down_hbm), (up, up_hbm), (embed, embed_hbm)]
        )
    ]
    for copy in arrivals:
        copy.start()
    for copy in arrivals:
        copy.wait()

    def take(halves, part, start, count):
        pieces, stop = [], start + count
        while start < stop:
            rank, row = start // CHUNK, start % CHUNK
            size = min(CHUNK - row, stop - start)
            at = part * CHUNK + row
            pieces.append(halves[rank // RANKS][rank % RANKS, at : at + size, :].astype(jnp.float32))
            start += size
        return pieces[0] if len(pieces) == 1 else jnp.concatenate(pieces, axis=0)

    def strip(i):
        return slice(i * LANES, (i + 1) * LANES)

    def unpack_head(halves):
        for i in range(D_T // LANES):
            head[:, strip(i)] = take(halves, 0, i * D_S, D_S)

    def unpack_down(halves):
        at = D_S * D_T // LANES
        for i in range(2):
            down[:, strip(i)] = take(halves, 0, at + i * S_HID, S_HID)
        down[:, 2 * LANES :] = take(halves, 1, 0, S_HID)

    def unpack_up(halves):
        for i in range(S_HID // LANES):
            up[:, strip(i)] = take(halves, 1, UP_AT + i * D_S, D_S)

    def unpack_rest(halves):
        for i in range(D_S // LANES):
            embed[:, strip(i)] = take(halves, 1, EMBED_AT + i * EMBED_ROWS, EMBED_ROWS)[:PIX]
        gains = take(halves, 1, GAIN_AT, 16)
        for i in range(D_S // LANES):
            gain[strip(i)] = gains[i]
        lane = lax.broadcasted_iota(jnp.int32, (1, LANES), 1)
        cosines = jnp.where(lane < 3, take(halves, 1, SUM_ROWS - 16, 16)[15:], 0.0)
        mean_distance[0] = 1.0 - jnp.sum(cosines) * (1.0 / (DEVICES * 2 * BLK))

    for unpack, copy in zip([unpack_head, unpack_down, unpack_up, unpack_rest], results):

        @pl.when(core[0] == 0)
        def _():
            unpack((mine, theirs))

        @pl.when(core[0] == 1)
        def _():
            unpack((theirs, mine))

        copy.start()
    for copy in results:
        copy.wait()


def unpack_sums(core, mine, theirs):
    smem, vmem, anywhere = [
        pl.BlockSpec(memory_space=space) for space in (pltpu.SMEM, pltpu.VMEM, pl.ANY)
    ]
    shapes = [(D_S, D_T), (S_HID, D_S), (D_S, S_HID), (PIX, D_S)]
    return pl.pallas_call(
        unpack_kernel,
        in_specs=[smem, anywhere, anywhere],
        out_specs=[anywhere] * 4 + [vmem, smem],
        out_shape=[jax.ShapeDtypeStruct(shape, jnp.float32) for shape in shapes + [(D_S,), (1,)]],
        scratch_shapes=[pltpu.VMEM(mine.shape, mine.dtype)] * 2
        + [pltpu.VMEM(shape, jnp.float32) for shape in shapes]
        + [pltpu.SemaphoreType.DMA((6,))],
        compiler_params=pltpu.CompilerParams(vmem_limit_bytes=24 * 1024 * 1024),
        cost_estimate=pl.CostEstimate(flops=0, bytes_accessed=12 * 1024 * 1024, transcendentals=0),
        name="unpack_sums",
    )(core, mine, theirs)


def core_sum(mine, theirs):
    return (mine + theirs).astype(jnp.bfloat16).reshape(RANKS, CHUNK, LANES)


def to_all_ranks(values):
    return lax.all_to_all(values, BOTH, 0, 0, axis_index_groups=core_groups(), tiled=True)


def chunk_kernel(owner, got, spread):
    chunk = jnp.sum(got[...].astype(jnp.float32), axis=0)
    lane = lax.broadcasted_iota(jnp.int32, (1, LANES), 1)
    parts = chunk[2 * CHUNK - 1 :, :]
    whole = jnp.sum(jnp.where(lane < 3, parts, 0.0), axis=1, keepdims=True)
    last = jnp.where(owner[0] == 1, three_parts(whole, lane), parts)
    rounded = jnp.concatenate([chunk[: 2 * CHUNK - 1, :], last], axis=0).astype(jnp.bfloat16)
    spread[...] = jnp.broadcast_to(rounded[None], spread.shape)


def add_chunk(owner, got):
    vmem = pl.BlockSpec(memory_space=pltpu.VMEM)
    return pl.pallas_call(
        chunk_kernel,
        in_specs=[pl.BlockSpec(memory_space=pltpu.SMEM), vmem],
        out_specs=vmem,
        out_shape=jax.ShapeDtypeStruct(got.shape, jnp.bfloat16),
        compiler_params=pltpu.CompilerParams(vmem_limit_bytes=32 * 1024 * 1024),
        cost_estimate=pl.CostEstimate(flops=0, bytes_accessed=4 * 1024 * 1024, transcendentals=0),
        name="add_chunk",
    )(owner, got)


def on_device(
    pixels,
    keyframes,
    destination,
    student_embed,
    student_gain,
    student_up,
    student_down,
    student_head,
    teacher_embed,
    teacher_gain,
    teacher_project,
    teacher_output,
):
    pool_size = lax.axis_size("pool")

    project = teacher_project[0].T
    embed_shard = jnp.pad(teacher_embed[0].T, ((0, 0), (0, D_T // 2 - PIX)))
    embed_shard = jnp.concatenate([embed_shard[:EMBED_PACK], embed_shard[EMBED_PACK:]], axis=1)
    gathered = lax.all_gather(
        jnp.concatenate([project[:CUT], embed_shard], axis=0), "student", axis=0, tiled=False
    )
    shard = jnp.concatenate([project[CUT:], teacher_output[0].T], axis=0)
    first = [moved(shard, z=1), moved(shard, x=1), moved(shard, x=-1)]

    owners = shard_owners()

    teachers = jnp.arange(pool_size, dtype=jnp.int32)[:, None, None]
    chosen = [
        lax.dynamic_index_in_dim(pixels, keyframes[0, k], 0, keepdims=True) for k in range(2)
    ]
    outgoing = jnp.where(
        destination[0, 0] == teachers,
        chosen[0],
        jnp.where(destination[0, 1] == teachers, chosen[1], jnp.zeros((), jnp.bfloat16)),
    )
    outgoing = jnp.pad(outgoing, ((0, 0), (0, 0), (0, PIX_PAD - PIX)))
    up, down, head = halves_of(student_up), halves_of(student_down), halves_of(student_head)
    embed = halves_of(jnp.pad(student_embed, ((0, PIX_PAD - PIX), (0, 0))))
    outgoing, up, down, head, embed, gain, *first = lax.optimization_barrier(
        (outgoing, up, down, head, embed, student_gain[None], *first)
    )
    across, back, ahead = first
    second = [
        moved(across, x=1), moved(across, x=-1), moved(back[:REST], x=1), moved(ahead[REST:], x=-1)
    ]
    arrived = lax.all_to_all(outgoing, "pool", split_axis=0, concat_axis=0, tiled=True)
    rows = arrived.reshape(pool_size * BLK, PIX_PAD)

    lifted = bf16_dot(rows, embed[0], NN) + bf16_dot(rows, embed[1], NN)
    normed_s = halves_of(lifted * rms_scale(lifted) * student_gain)
    pre = halved_dot(normed_s, up)
    cdf = 0.5 * (1.0 + lax.erf(pre * (2.0**-0.5)))
    act = halves_of(pre * cdf)
    slope = cdf + pre * jnp.exp(-0.5 * pre * pre) * ((2.0 * jnp.pi) ** -0.5)
    act, slope, *second = lax.optimization_barrier((act, slope, *second))
    back_across, ahead_across, low_near, high_near = second
    third = [moved(back_across[:REST], x=1), moved(ahead_across[REST:], x=-1)]
    near = with_core([shard, across, back, back_across, ahead, ahead_across])
    hidden = halves_of(lifted + halved_dot(act, down))
    student_out = halved_dot(hidden, head)
    student_out, *third = lax.optimization_barrier((student_out, *third))
    low = with_core([low_near, third[0]])
    high = with_core([high_near, third[1]])

    core = lax.rem(lax.axis_index("student"), 2).reshape(1)
    *sums_a, down_rest, d_hidden, total = teacher_and_head(
        core, owners, rows, teacher_gain, gathered, near + low, high, student_out, hidden, act, head
    )
    theirs_a = core_swap(sums_a[1])
    sums_b = trunk_backward(
        core, d_hidden, slope, down, up, normed_s, lifted, gain, rows, down_rest, total
    )
    rank = lax.axis_index("student") // 2 * 8 + lax.axis_index("pool")
    owner = jnp.logical_and(core == 1, rank == RANKS - 1).astype(jnp.int32)
    theirs_a, *sums_b = lax.optimization_barrier((theirs_a, *sums_b))
    sent = [core_sum(sums_a[0], theirs_a), core_sum(sums_b[0], core_swap(sums_b[1]))]
    got = to_all_ranks(jnp.concatenate(sent, axis=1))
    half = to_all_ranks(add_chunk(owner, got))
    head_sum, down_sum, up_sum, embed_sum, gain_sum, mean_distance = unpack_sums(
        core, half, core_swap(half)
    )
    return (mean_distance.reshape(()), embed_sum, gain_sum, up_sum, down_sum, head_sum)


def solution(mesh):
    in_specs = (
        P(("student", "pool"), None, None),
        P(("student", "pool"), None),
        P(("student", "pool"), None),
        P(),
        P(),
        P(),
        P(),
        P(),
        P("pool", None, "student"),
        P("pool", None),
        P("pool", None, "student"),
        P("pool", None, "student"),
    )
    out_specs = (P(), P(), P(), P(), P(), P())
    return jax.shard_map(
        on_device, mesh=mesh, in_specs=in_specs, out_specs=out_specs, check_vma=False
    )
```
